512 devices in a mesh: section: 4 (over x_lo, core), dp: 8 (over z), tensor: 16 (over x_hi, y).
Axes of the slice: x: 4 (x_hi: 2, x_lo: 2; x = x_hi * 2 + x_lo), y: 8, z: 8, core: 2. Of those that a mesh axis runs over, the one named last changes fastest.
Arguments:
- resid_in: bfloat16 [4, 1024, 8192], P('section', ('dp', 'tensor')), may hold values from -6 to 6
- attn_in: bfloat16 [4, 1024, 12288], P('section', 'dp', 'tensor'), may hold values from -22 to 22, as said below
- seg_fwd: int32 [4, 8, 128], P('section', 'dp'), may hold values from 0 to 7, never falling along the last dimension, each value on 1 to 48 neighbouring positions
- out_weight: bfloat16 [4, 8192, 8192], P('section', 'tensor', 'dp'), may hold values from -0.0625 to 0.0625
- stash_held: bfloat16 [4, 3, 1024, 20480], P('section', None, 'dp', 'tensor'), may hold values from -22 to 22, as said below
- len_bwd: int32 [4, 8, 8], P('section', 'dp'), may hold values from 1 to 48, 128 in all within a row
- out_grad: bfloat16 [4, 1024, 8192], P('section', ('dp', 'tensor')), may hold values from -6 to 6
- evict_slot: int32 [4], P('section'), may hold values from 0 to 2
- fetch_slot: int32 [4, 8], P('section', 'dp'), may hold values from 0 to 2
Outputs:
- layer_out: bfloat16 [4, 1024, 8192], P('section', ('dp', 'tensor'))
- stash_next: bfloat16 [4, 3, 1024, 20480], P('section', None, 'dp', 'tensor')
- weight_grad: bfloat16 [4, 8192, 8192], P('section', 'tensor', 'dp')
- attn_grad: bfloat16 [4, 1024, 12288], P('section', 'dp', 'tensor')
The draws below stay inside these ranges and needn't reach their ends.
Inputs may be any that keep to these rules, and one draw needn't show every extreme that they name: `attn_in`: the blocks of one group hold equal keys and equal values. `stash_held`: the blocks of one group hold equal keys and equal values. `seg_fwd`: each run of 128 tokens holds 8 sequences, the longest exactly 48 tokens. `len_bwd`: each run's lengths sum to 128, the largest exactly 48.
All inputs are finite; a program needn't handle non-finite values.
Results may differ from the reference program's by a relative error of at most 0.02.
Values may be sent and summed in bfloat16 or wider, within the bound.
A program may use at most 64 MiB of HBM per device.

```python
import math
import jax
import jax.numpy as jnp
import numpy as np
from jax import lax

D = 8192
HEADS = 64
KV_HEADS = 8
HEAD = 128
TOK_DEV = 128
SEQS = 8
SLOTS = 3
SECTIONS = 4
TOKENS = 1024
Q_DEV = 4
KV_DEV = 1
GROUP_DEV = 2
W_DEV = 768
SW_DEV = 1280
N_DP = 8
N_TENSOR = 16


def aligned_heads(key, leading, head_slots, picked_of_64):
    group_size = max(1, HEADS // KV_HEADS // Q_DEV)
    leader = np.arange(N_TENSOR) // group_size * group_size
    slot_index = np.arange(head_slots).reshape(1, 1, 1, head_slots, 1)
    shared_slots = jnp.asarray((slot_index >= Q_DEV) & (slot_index < Q_DEV + 2 * KV_DEV))
    base = jnp.clip(jax.random.normal(jax.random.fold_in(key, 1), (leading, TOKENS, N_TENSOR, head_slots, HEAD), jnp.float32), -5.0, 5.0)
    base = jnp.where(shared_slots, base[:, :, leader], base)
    picked = jax.random.randint(jax.random.fold_in(key, 2), (leading, TOKENS, N_TENSOR, 1, 1), 0, 64) < picked_of_64
    picked = picked[:, :, leader]
    level = 3.0 + 0.65 * jax.random.randint(jax.random.fold_in(key, 3), (leading, TOKENS, N_TENSOR, 1, 1), 0, 3).astype(jnp.float32)
    level = level[:, :, leader]
    aligned = level * base[:, :, :, Q_DEV:Q_DEV + 1, :]
    aligned_next = jnp.roll(aligned, -1, axis=1)
    picked_next = jnp.roll(picked, -1, axis=1)
    query_slots = jnp.asarray(slot_index < Q_DEV // KV_DEV)
    key_slot = jnp.asarray(slot_index == Q_DEV)
    result = jnp.where(picked & (query_slots | key_slot), aligned, base)
    result = jnp.where(picked_next & key_slot & jnp.logical_not(picked), 0.985 * aligned_next, result)
    return result


def draw_attn_in(key, part):
    key = jax.random.fold_in(key, 11)
    picked_of_64 = 0
    values = aligned_heads(key, SECTIONS, W_DEV // HEAD, picked_of_64)
    return values.reshape(SECTIONS, TOKENS, N_TENSOR * W_DEV).astype(jnp.bfloat16)


def draw_stash_held(key, part):
    key = jax.random.fold_in(key, 23)
    picked_of_64 = 0
    values = aligned_heads(key, SECTIONS * SLOTS, SW_DEV // HEAD, picked_of_64)
    return values.reshape(SECTIONS, SLOTS, TOKENS, N_TENSOR * SW_DEV).astype(jnp.bfloat16)


def with_ends(drawn, stream_key, least, top_value):
    longest = drawn.shape.index(max(drawn.shape))
    spots = []
    for shift in (0, 1):
        where = [jax.random.randint(jax.random.fold_in(stream_key, axis), (), 0, length) for axis, length in enumerate(drawn.shape)]
        where[longest] = (where[longest] + shift) % drawn.shape[longest]
        spots.append(tuple(where))
    return drawn.at[spots[0]].set(least).at[spots[1]].set(top_value)


def block_levels(key, shape, shards, smallest, top_value):
    loudness = 1.0
    for dim, shards_of in shards:
        heights = jax.random.uniform(jax.random.fold_in(jax.random.fold_in(key, 6), dim), (shards_of,), jnp.float32, smallest / len(shards), top_value / len(shards))
        loudness = loudness * jnp.repeat(jnp.exp(heights), shape[dim] // shards_of).reshape((-1,) + (1,) * (len(shape) - 1 - dim))
    return loudness


def profile(amount, total, bound, skew):
    portions = [(1 << 20) // math.isqrt(standing ** skew) + 1 for standing in range(2, amount + 1)]
    spare, counts = total - bound - (amount - 1), [1] * (amount - 1)
    while spare > 0:
        movable = [i for i in range(amount - 1) if counts[i] < bound]
        whole, budget = sum([portions[i] for i in movable]), spare
        for i in movable:
            extra = min(bound - counts[i], max(1, budget * portions[i] // whole), spare)
            counts[i] = counts[i] + extra
            spare = spare - extra
    return np.array([bound] + counts)


def uneven_parts(own_key, amount, total, limit, lean):
    if amount == 2:
        one = jax.random.randint(own_key, (), max(1, total - limit), min(limit, total - 1) + 1)
        return jnp.stack([one, total - one])
    sizes = jnp.asarray(profile(amount, total, limit, lean), jnp.int32)
    pairs = (amount - 1) // 2
    giver, taker = sizes[1:1 + 2 * pairs:2], sizes[2:2 + 2 * pairs:2]
    slack = jnp.minimum(giver - 1, limit - taker)
    passed = jax.random.randint(jax.random.fold_in(own_key, 1), (pairs,), 0, 1 << 20) % (slack + 1)
    sizes = sizes.at[1:1 + 2 * pairs:2].set(giver - passed).at[2:2 + 2 * pairs:2].set(taker + passed)
    return sizes[jax.random.permutation(jax.random.fold_in(own_key, 2), amount)]


def gaussian(stream_key, extent, spread, bound, split=(), kind=jnp.bfloat16):
    drawn = jax.random.normal(stream_key, extent, jnp.float32) * spread
    if len(split) > 0:
        drawn = block_levels(stream_key, extent, split, -0.22, 0.18) * drawn
    return jnp.clip(drawn, min=-bound, max=bound).astype(kind)


def setup_inputs(seed: int = 0) -> dict:
    keys = jax.random.split(jax.random.key(seed), 10)
    return {
        "resid_in": gaussian(keys[0], (SECTIONS, TOKENS, D), 0.5, 6.0, ((0, 4), (1, 128))),
        "attn_in": draw_attn_in(jax.random.fold_in(keys[9], 71), 0),
        "seg_fwd": jax.vmap(lambda own: jnp.searchsorted(jnp.cumsum(uneven_parts(own, SEQS, TOK_DEV, 3 * TOK_DEV // SEQS, 2)), jnp.arange(TOK_DEV), side="right"))(jax.random.split(keys[2], SECTIONS * N_DP)).reshape((SECTIONS, N_DP, TOK_DEV)).astype(jnp.int32),
        "out_weight": gaussian(keys[3], (SECTIONS, HEADS * HEAD, D), (HEADS * HEAD) ** -0.5, 0.0625, ((0, 4), (1, 16), (2, 8))),
        "stash_held": draw_stash_held(jax.random.fold_in(keys[9], 71), 0),
        "len_bwd": jax.vmap(lambda own: uneven_parts(own, SEQS, TOK_DEV, 3 * TOK_DEV // SEQS, 2))(jax.random.split(keys[5], SECTIONS * N_DP)).reshape((SECTIONS, N_DP, SEQS)).astype(jnp.int32),
        "out_grad": gaussian(keys[6], (SECTIONS, TOKENS, D), 1.0, 6.0, ((0, 4), (1, 128))),
        "evict_slot": with_ends(jax.random.randint(keys[7], (SECTIONS,), 0, SLOTS), jax.random.fold_in(keys[7], 1), 0, SLOTS - 1).astype(jnp.int32),
        "fetch_slot": with_ends(jax.random.randint(keys[8], (SECTIONS, N_DP), 0, SLOTS), jax.random.fold_in(keys[8], 1), 0, SLOTS - 1).astype(jnp.int32),
    }


def split_heads(packed):
    tok_count = packed.shape[0]
    q_width = Q_DEV * HEAD
    kv_width = KV_DEV * HEAD
    query_heads = packed[:, :q_width].reshape(tok_count, KV_DEV, Q_DEV // KV_DEV, HEAD).astype(jnp.float32)
    key_heads = packed[:, q_width:q_width + kv_width].reshape(tok_count, KV_DEV, HEAD).astype(jnp.float32)
    value_heads = packed[:, q_width + kv_width:q_width + 2 * kv_width].reshape(tok_count, KV_DEV, HEAD).astype(jnp.float32)
    return query_heads, key_heads, value_heads


def probabilities(query_heads, key_heads, segment):
    scores = jnp.einsum("tkgd,skd->kgts", query_heads, key_heads) * (HEAD ** -0.5)
    tok_count = segment.shape[0]
    position = jnp.arange(tok_count, dtype=jnp.int32)
    allowed = (segment[:, None] == segment[None, :]) & (position[None, :] <= position[:, None])
    masked = jnp.where(allowed, scores, -1e30)
    highest = jnp.max(masked, axis=-1, keepdims=True)
    raised = jnp.where(allowed, jnp.exp(masked - highest), 0.0)
    return raised / jnp.sum(raised, axis=-1, keepdims=True)


def attend(packed, segment):
    query_heads, key_heads, value_heads = split_heads(packed)
    weights = probabilities(query_heads, key_heads, segment).astype(jnp.bfloat16).astype(jnp.float32)
    result = jnp.einsum("kgts,skd->tkgd", weights, value_heads)
    return result.astype(jnp.bfloat16).reshape(packed.shape[0], Q_DEV * HEAD)


def attend_back(packed, segment, grad_out):
    tok_count = packed.shape[0]
    query_heads, key_heads, value_heads = split_heads(packed)
    outputs = packed[:, W_DEV:].reshape(tok_count, KV_DEV, Q_DEV // KV_DEV, HEAD).astype(jnp.float32)
    probs = probabilities(query_heads, key_heads, segment)
    weights = probs.astype(jnp.bfloat16).astype(jnp.float32)
    grad_heads = grad_out.reshape(tok_count, KV_DEV, Q_DEV // KV_DEV, HEAD).astype(jnp.float32)
    grad_values = jnp.einsum("kgts,tkgd->skd", weights, grad_heads)
    grad_probs = jnp.einsum("tkgd,skd->kgts", grad_heads, value_heads)
    inner = jnp.transpose(jnp.sum(grad_heads * outputs, axis=-1), (1, 2, 0))[..., None]
    grad_scores = (probs * (grad_probs - inner)).astype(jnp.bfloat16).astype(jnp.float32)
    grad_query = jnp.einsum("kgts,skd->tkgd", grad_scores, key_heads) * (HEAD ** -0.5)
    grad_keys = jnp.einsum("kgts,tkgd->skd", grad_scores, query_heads) * (HEAD ** -0.5)
    shared = jnp.concatenate([grad_keys.reshape(tok_count, KV_DEV * HEAD), grad_values.reshape(tok_count, KV_DEV * HEAD)], axis=1)
    return grad_query.astype(jnp.bfloat16).reshape(tok_count, Q_DEV * HEAD), shared


def lengths_to_segments(lengths):
    ends = jnp.cumsum(lengths).astype(jnp.int32)
    position = jnp.arange(TOK_DEV, dtype=jnp.int32)
    return jnp.sum((position[:, None] >= ends[None, :]).astype(jnp.int32), axis=1).astype(jnp.int32)


def reference(resid_in, attn_in, seg_fwd, out_weight, stash_held, len_bwd, out_grad, evict_slot, fetch_slot):
    q_width = Q_DEV * HEAD
    layer_list, evicted_list, wgrad_list, agrad_list = [], [], [], []
    for section in range(SECTIONS):
        blocks = attn_in[section].reshape(N_DP, TOK_DEV, N_TENSOR, W_DEV).transpose(0, 2, 1, 3)
        outputs = jax.vmap(jax.vmap(attend, (0, None)), (0, 0))(blocks, seg_fwd[section])
        branch = jnp.zeros((TOKENS, D), jnp.float32)
        for part in range(N_TENSOR):
            rows = outputs[:, part].reshape(TOKENS, q_width)
            term = jnp.dot(rows, out_weight[section, part * q_width:(part + 1) * q_width], preferred_element_type=jnp.float32)
            branch = branch + lax.optimization_barrier(term.astype(jnp.bfloat16)).astype(jnp.float32)
        layer_list.append((resid_in[section].astype(jnp.float32) + branch).astype(jnp.bfloat16))
        evicted = jnp.concatenate([blocks, outputs], axis=3).transpose(0, 2, 1, 3).reshape(TOKENS, N_TENSOR * SW_DEV)
        evicted_list.append(evicted)
    next_list = []
    for section in range(SECTIONS):
        mirror = section ^ (SECTIONS - 1)
        slot_index = jnp.arange(SLOTS, dtype=jnp.int32)[:, None, None]
        next_list.append(jnp.where(slot_index == evict_slot[section], evicted_list[mirror][None], stash_held[section]))
        held_runs = stash_held[mirror].reshape(SLOTS, N_DP, TOK_DEV, N_TENSOR * SW_DEV)
        run_list = []
        for run in range(N_DP):
            run_list.append(lax.dynamic_index_in_dim(held_runs[:, run], fetch_slot[mirror, run], 0, keepdims=False))
        returned = jnp.stack(run_list, 0).reshape(TOKENS, N_TENSOR * SW_DEV)
        back_blocks = returned.reshape(N_DP, TOK_DEV, N_TENSOR, SW_DEV).transpose(0, 2, 1, 3)
        segments = jax.vmap(lengths_to_segments)(len_bwd[section])
        grad = out_grad[section]
        head_list, wrows = [], []
        for part in range(N_TENSOR):
            weight_part = out_weight[section, part * q_width:(part + 1) * q_width]
            head_list.append(jnp.dot(grad, weight_part.T, preferred_element_type=jnp.float32).astype(jnp.bfloat16))
            old_outputs = back_blocks[:, part, :, W_DEV:].reshape(TOKENS, q_width)
            wrows.append(jnp.dot(old_outputs.T, grad, preferred_element_type=jnp.float32).astype(jnp.bfloat16))
        wgrad_list.append(jnp.concatenate(wrows, axis=0))
        head_grad = jnp.stack(head_list, 0).reshape(N_TENSOR, N_DP, TOK_DEV, q_width).transpose(1, 0, 2, 3)
        grad_query, shared = jax.vmap(jax.vmap(attend_back, (0, None, 0)), (0, 0, 0))(back_blocks, segments, head_grad)
        grouped = shared.reshape(N_DP, N_TENSOR // GROUP_DEV, GROUP_DEV, TOK_DEV, 2 * KV_DEV * HEAD)
        grouped = jnp.broadcast_to(jnp.sum(grouped, axis=2, keepdims=True), grouped.shape)
        shared_grad = grouped.reshape(N_DP, N_TENSOR, TOK_DEV, 2 * KV_DEV * HEAD).astype(jnp.bfloat16)
        grads = jnp.concatenate([grad_query, shared_grad], axis=3)
        agrad_list.append(grads.transpose(0, 2, 1, 3).reshape(TOKENS, N_TENSOR * W_DEV))
    return (jnp.stack(layer_list, 0), jnp.stack(next_list, 0), jnp.stack(wgrad_list, 0), jnp.stack(agrad_list, 0))
```

```python
import functools

import jax
import jax.numpy as jnp
from jax import lax
from jax.experimental import pallas as pl
from jax.experimental.pallas import tpu as pltpu
from jax.sharding import PartitionSpec as P

HEAD = 128
ROWS = 8
MESH = pl.DeviceIdType.MESH
F32 = jnp.float32
BF16 = jnp.bfloat16
SEMS = 128


def dot(a, b, ca=1, cb=0):
    return lax.dot_general(a, b, (((ca,), (cb,)), ((), ())), preferred_element_type=F32)


def streams(n):
    h = n // 2
    return [s for s in ((1, 0, h), (-1, 1, h), (1, 1, h - 1), (-1, 0, h - 1)) if s[2] > 0]


def probabilities(q, k, allowed, heads):
    tok = k.shape[0]
    scores = dot(q, k, 1, 1).reshape(heads, tok, tok) * HEAD ** (-0.5)
    masked = jnp.where(allowed[None], scores, -1e30)
    highest = jnp.max(masked, axis=-1, keepdims=True)
    raised = jnp.where(allowed[None], jnp.exp(masked - highest), 0.0)
    return (raised / jnp.sum(raised, axis=-1, keepdims=True)).reshape(heads * tok, tok)


def stack_heads(x, heads):
    return jnp.concatenate([x[:, h * HEAD : (h + 1) * HEAD] for h in range(heads)], axis=0)


def unstack_heads(x, heads):
    tok = x.shape[0] // heads
    return jnp.concatenate([x[h * tok : (h + 1) * tok] for h in range(heads)], axis=1)


def to_tall(x):
    half = x.shape[1] // 2
    return jnp.concatenate([x[:, :half], x[:, half:]], axis=0)


def to_wide(x):
    return jnp.concatenate([x[:ROWS], x[ROWS:]], axis=1)


class Copies:
    def __init__(self, send_sems, recv_sems):
        self.send_sems, self.recv_sems = send_sems, recv_sems
        self.count = 0
        self.started = []

    def make(self, src, dst, device):
        i = self.count
        self.count += 1
        assert i < SEMS
        return pltpu.make_async_remote_copy(
            src_ref=src,
            dst_ref=dst,
            send_sem=self.send_sems.at[i],
            recv_sem=self.recv_sems.at[i],
            device_id=device,
            device_id_type=MESH,
        )

    def send(self, src, dst, device):
        copy = self.make(src, dst, device)
        copy.start()
        self.started.append(copy)
        return copy

    def finish(self):
        for copy in self.started:
            copy.wait_send()


class Gather:
    def __init__(self, copies, n, me, device, place):
        self.copies, self.n, self.me = copies, n, me
        self.device, self.place = device, place
        self.streams = streams(n)
        self.moves = {}

    def step(self, r, halves=(0, 1)):
        for half in halves:
            for way, h, hops in self.streams:
                if h != half:
                    continue
                if 1 <= r <= hops:
                    self.moves[(way, h, r - 1)].wait_recv()
                if r < hops:
                    origin = (self.me - way * r + self.n) % self.n
                    ref = self.place(origin, h)
                    to = (self.me + way + self.n) % self.n
                    self.moves[(way, h, r)] = self.copies.send(ref, ref, self.device(to))


class Reduce:
    def __init__(self, copies, n, me, device, slots):
        self.copies, self.n, self.me = copies, n, me
        self.device, self.slots = device, slots
        self.streams = streams(n)
        self.h = n // 2
        self.moves = {}

    def slot(self, way, half, r):
        return self.slots.at[0 if way == 1 else 1, half, r]

    def step(self, r, own):
        for way, half, hops in self.streams:
            first = self.h - hops
            if r < first:
                continue
            ref = self.slot(way, half, r)
            value = own(way, half)
            if r > first:
                self.moves[(way, half, r - 1)].wait_recv()
                value = value + ref[...].astype(F32)
            ref[...] = value.astype(BF16)
            to = (self.me + way + self.n) % self.n
            self.moves[(way, half, r)] = self.copies.send(
                ref, self.slot(way, half, r + 1), self.device(to)
            )

    def last(self, half):
        total = None
        for way, h, hops in self.streams:
            if h != half:
                continue
            self.moves[(way, h, self.h - 1)].wait_recv()
            part = self.slot(way, h, self.h)[...].astype(F32)
            total = part if total is None else total + part
        return total


def kernel(
    dims,
    resid,
    attn_in,
    seg,
    lens,
    weight_hbm,
    stash_hbm,
    out_grad,
    evict,
    fetch,
    lay_out,
    stash_out,
    wgrad_out,
    agrad_out,
    weight,
    stash,
    b1s,
    b1r,
    G,
    part,
    zslots,
    A,
    O,
    yslots,
    xs,
    xr,
    f5s,
    f5r,
    attb,
    reto,
    retq,
    retr,
    evp,
    eva,
    shs,
    shr,
    OT,
    wgv,
    send_sems,
    recv_sems,
    local_sems,
):
    n_sec, nz, nt = dims
    ny = nt // 2
    tok = nt * ROWS
    C = weight.shape[1]
    QW = weight.shape[0]
    heads = QW // HEAD
    W_IN = QW + 2 * HEAD

    sec = lax.axis_index("section")
    z = lax.axis_index("dp")
    t = lax.axis_index("tensor")
    xh = t // ny
    y = t % ny
    mirror = {"section": n_sec - 1 - sec}
    xpeer = {"tensor": (1 - xh) * ny + y}
    pair = {"tensor": t + 1 - 2 * (t % 2)}

    def zdev(i):
        return {"dp": i}

    def ydev(i):
        return {"tensor": xh * ny + i}

    barrier = pltpu.get_barrier_semaphore()
    greeted = [zdev((z + k) % nz) for k in range(1, nz)]
    greeted += [ydev((y + 1) % ny), ydev((y + ny - 1) % ny)] + [xpeer, mirror]
    for device in greeted:
        pl.semaphore_signal(barrier, inc=1, device_id=device, device_id_type=MESH)

    load_weight = pltpu.make_async_copy(weight_hbm, weight, local_sems.at[0])
    load_stash = pltpu.make_async_copy(stash_hbm, stash, local_sems.at[1])
    load_stash.start()
    load_weight.start()

    copies = Copies(send_sems, recv_sems)

    for d in range(nz):
        b1s[d] = to_tall(out_grad[:, d * C : (d + 1) * C].astype(F32)).astype(BF16)
    b1r[z] = b1s[z]

    pl.semaphore_wait(barrier, len(greeted))

    b1 = []
    for k in range(1, nz):
        d = (z + k) % nz
        b1.append(copies.send(b1s.at[d], b1r.at[z], zdev(d)))

    def permuted(x):
        return [
            jnp.concatenate(
                [x[h * ny * ROWS + b * ROWS : h * ny * ROWS + (b + 1) * ROWS] for h in (0, 1)],
                axis=0,
            )
            for b in range(ny)
        ]

    def natural(x):
        return jnp.concatenate(
            [x[(2 * b + h) * ROWS : (2 * b + h + 1) * ROWS] for h in (0, 1) for b in range(ny)],
            axis=0,
        )

    load_stash.wait()
    slot = fetch[0, 0]
    held = stash[slot]
    for b, rows in enumerate(permuted(held[:, W_IN:].astype(F32))):
        reto[b] = rows.astype(BF16)
    retq[...] = held[:, :W_IN]
    move_ret_o = copies.send(reto, O.at[:, z], mirror)

    row_id = lax.broadcasted_iota(jnp.int32, (tok, tok), 0)
    col_id = lax.broadcasted_iota(jnp.int32, (tok, tok), 1)
    seg_cols = jnp.broadcast_to(seg[...].astype(F32), (tok, tok))
    allowed = (seg_cols == jnp.transpose(seg_cols)) & (col_id <= row_id)
    q = stack_heads(attn_in[:, :QW], heads)
    k = attn_in[:, QW : QW + HEAD]
    v = attn_in[:, QW + HEAD : W_IN]
    weights = probabilities(q, k, allowed, heads).astype(BF16)
    att = unstack_heads(dot(weights, v), heads)
    attb[...] = att.astype(BF16)
    for b, rows in enumerate(permuted(att)):
        A[b, z] = rows.astype(BF16)

    hy = ny // 2
    gather_a = Gather(copies, nz, z, zdev, lambda o, h: A.at[pl.ds(h * hy, hy), o])
    gather_o = Gather(copies, nz, z, zdev, lambda o, h: O.at[pl.ds(h * hy, hy), o])
    gather_g = Gather(copies, ny, y, ydev, lambda o, h: G.at[o, xh if h == 0 else 1 - xh])
    reduce_z = Reduce(copies, nz, z, zdev, zslots)
    reduce_y = Reduce(copies, ny, y, ydev, yslots)

    gather_a.step(0)

    for copy in b1:
        copy.wait_recv()
    for p in range(nz // 2):
        rows = [to_wide(b1r[2 * p + j].astype(F32)) for j in (0, 1)]
        G[y, xh, pl.ds(2 * ROWS * p, 2 * ROWS), :] = jnp.concatenate(rows, axis=0).astype(BF16)
    move_g = copies.send(G.at[y, xh], G.at[y, xh], xpeer)
    gather_g.step(0, (0,))
    move_g.wait_recv()
    gather_g.step(0, (1,))

    move_ret_q = copies.send(retq, retr, mirror)
    move_ev_p = copies.send(attn_in, evp, mirror)
    move_ev_a = copies.send(attb, eva, mirror)
    load_weight.wait()

    def head_grad_part(b):
        res = dot(G[b].reshape(2 * nz * ROWS, C), weight[...], 1, 1)
        for d in range(nz):
            pair_rows = [res[(h * nz + d) * ROWS : (h * nz + d + 1) * ROWS] for h in (0, 1)]
            part[d, b] = jnp.concatenate(pair_rows, axis=0).astype(BF16)

    def branch_part(b):
        return dot(A[b].reshape(2 * nz * ROWS, QW), weight[...])

    def at_y(way, r):
        return (y + way * r + ny) % ny

    def at_z(way, r):
        return (z + way * r + nz) % nz

    def head_grad_step(r):
        def own(way, half):
            return part[at_z(way, nz // 2 - r), pl.ds(half * hy, hy)].astype(F32)

        reduce_z.step(r, own)

    half_rows = nz * ROWS

    def branch_step(r):
        parts = {1: branch_part(at_y(1, hy - r))}
        parts[-1] = branch_part(at_y(-1, hy - r)) if r > 0 else parts[1]

        def own(way, half):
            return parts[way][half * half_rows : (half + 1) * half_rows]

        reduce_y.step(r, own)

    hz = nz // 2
    head_grad_part(y)
    gather_a.step(1)
    move_ret_o.wait_recv()
    gather_o.step(0)
    for r in range(1, hy):
        gather_g.step(r)
        if r + 1 <= hz:
            gather_a.step(r + 1)
        if r <= hz:
            gather_o.step(r)
        head_grad_part(at_y(1, r))
        head_grad_part(at_y(-1, r))
    for r in range(hy + 1, hz + 1):
        gather_a.step(r)
    branch_step(0)
    for r in range(hy, hz + 1):
        gather_o.step(r)
    gather_g.step(hy)
    head_grad_part(at_y(1, hy))

    def weight_grad_part(i):
        cols = pl.ds(i * (C // 4), C // 4)
        wgv[:, cols] = dot(OT[...], G[:, :, :, cols].reshape(nt * nz * ROWS, C // 4)).astype(BF16)

    def arrange_outputs():
        for b in range(ny):
            x = O[b].astype(F32)
            rows = [x[d, h * ROWS : (h + 1) * ROWS] for h in (0, 1) for d in range(nz)]
            block = jnp.concatenate(rows, axis=0)
            width = 2 * nz * ROWS
            OT[:, b * width : (b + 1) * width] = jnp.transpose(block).astype(BF16)

    head_grad_step(0)
    arrange_outputs()
    for r in range(1, max(hy, hz)):
        if r < hz:
            head_grad_step(r)
        if r < hy:
            branch_step(r)
        weight_grad_part(r - 1)
    for i in range(max(hy, hz) - 1, 4):
        weight_grad_part(i)
    store_wgrad = pltpu.make_async_copy(wgv, wgrad_out, local_sems.at[2])
    store_wgrad.start()

    halves = []
    for h in (0, 1):
        own = part[z, pl.ds(h * hy, hy)].astype(F32)
        halves.append((own + reduce_z.last(h)).reshape(hy * 2 * ROWS, QW))
    d_out = natural(jnp.concatenate(halves, axis=0)).astype(BF16)
    old = natural(O[:, z].astype(F32).reshape(tok, QW))
    move_ret_q.wait_recv()
    end = jnp.int32(0)
    seg_row = jnp.zeros((tok, tok), jnp.int32)
    seg_col = jnp.zeros((tok, tok), jnp.int32)
    for c in range(lens.shape[1]):
        end = end + lens[0, c]
        seg_row += (row_id >= end).astype(jnp.int32)
        seg_col += (col_id >= end).astype(jnp.int32)
    allowed = (seg_row == seg_col) & (col_id <= row_id)
    q = stack_heads(retr[:, :QW], heads)
    k = retr[:, QW : QW + HEAD]
    v = retr[:, QW + HEAD : W_IN]
    probs = probabilities(q, k, allowed, heads)
    d_heads = stack_heads(d_out, heads)
    grad_v = dot(probs.astype(BF16), d_heads, 0, 0)
    grad_p = dot(d_heads, v, 1, 1)
    inner = jnp.sum(d_heads.astype(F32) * stack_heads(old, heads), axis=-1, keepdims=True)
    grad_s = (probs * (grad_p - inner)).astype(BF16)
    grad_k = dot(grad_s, q, 0, 0) * HEAD ** (-0.5)
    shs[:, :HEAD] = grad_k.astype(BF16)
    shs[:, HEAD:] = grad_v.astype(BF16)
    move_shared = copies.send(shs, shr, pair)
    grad_q = dot(grad_s, k) * HEAD ** (-0.5)
    agrad_out[:, :QW] = unstack_heads(grad_q, heads).astype(BF16)

    mine = branch_part(y)
    sums = [mine[h * half_rows : (h + 1) * half_rows] + reduce_y.last(h) for h in (0, 1)]
    total = jnp.concatenate(sums, axis=0)

    def of_half(h):
        return jnp.concatenate(
            [total[(2 * d + h) * ROWS : (2 * d + h + 1) * ROWS] for d in range(nz)], axis=0
        )

    low, high = of_half(0), of_half(1)
    xs[...] = jnp.where(xh == 0, high, low).astype(BF16)
    move_x = copies.send(xs, xr, xpeer)
    keep = jnp.where(xh == 0, low, high)

    move_ev_p.wait_recv()
    move_ev_a.wait_recv()
    for i in range(stash.shape[0]):
        here = evict[0] == i
        stash[i, :, :W_IN] = jnp.where(here, evp[...], stash[i, :, :W_IN])
        stash[i, :, W_IN:] = jnp.where(here, eva[...], stash[i, :, W_IN:])
    store_stash = pltpu.make_async_copy(stash, stash_out, local_sems.at[3])
    store_stash.start()

    move_x.wait_recv()
    keep = keep + xr[...].astype(F32)
    for d in range(nz):
        f5s[d] = to_tall(keep[d * ROWS : (d + 1) * ROWS]).astype(BF16)
    f5r[z] = f5s[z]
    f5 = []
    for kk in range(1, nz):
        d = (z + kk) % nz
        f5.append(copies.send(f5s.at[d], f5r.at[z], zdev(d)))

    move_shared.wait_recv()
    agrad_out[:, QW:] = (shs[...].astype(F32) + shr[...].astype(F32)).astype(BF16)

    for copy in f5:
        copy.wait_recv()
    for d in range(nz):
        cols = slice(d * C, (d + 1) * C)
        lay_out[:, cols] = (resid[:, cols].astype(F32) + to_wide(f5r[d].astype(F32))).astype(BF16)

    copies.finish()
    store_wgrad.wait()
    store_stash.wait()


def body(
    dims,
    resid_in,
    attn_in,
    seg_fwd,
    out_weight,
    stash_held,
    len_bwd,
    out_grad,
    evict_slot,
    fetch_slot,
):
    n_sec, nz, nt = dims
    ny = nt // 2
    tok = nt * ROWS
    QW, C = out_weight.shape[1:]
    D = resid_in.shape[-1]
    W_IN = QW + 2 * HEAD
    slots, width = stash_held.shape[1], stash_held.shape[-1]
    vmem, smem, anywhere = (
        pl.BlockSpec(memory_space=s) for s in (pltpu.VMEM, pltpu.SMEM, pl.ANY)
    )

    def buf(*shape):
        return pltpu.VMEM(shape, BF16)

    outs = pl.pallas_call(
        functools.partial(kernel, dims),
        out_shape=(
            jax.ShapeDtypeStruct((ROWS, D), BF16),
            jax.ShapeDtypeStruct((slots, tok, width), BF16),
            jax.ShapeDtypeStruct((QW, C), BF16),
            jax.ShapeDtypeStruct((tok, W_IN), BF16),
        ),
        in_specs=[vmem, vmem, vmem, smem, anywhere, anywhere, vmem, smem, smem],
        out_specs=(vmem, anywhere, anywhere, vmem),
        scratch_shapes=[
            buf(QW, C),
            buf(slots, tok, width),
            buf(nz, 2 * ROWS, C // 2),
            buf(nz, 2 * ROWS, C // 2),
            buf(ny, 2, nz * ROWS, C),
            buf(nz, ny, 2 * ROWS, QW),
            buf(2, 2, nz // 2 + 1, ny // 2, 2 * ROWS, QW),
            buf(ny, nz, 2 * ROWS, QW),
            buf(ny, nz, 2 * ROWS, QW),
            buf(2, 2, ny // 2 + 1, nz * ROWS, C),
            buf(nz * ROWS, C),
            buf(nz * ROWS, C),
            buf(nz, 2 * ROWS, C // 2),
            buf(nz, 2 * ROWS, C // 2),
            buf(tok, QW),
            buf(ny, 2 * ROWS, QW),
            buf(tok, W_IN),
            buf(tok, W_IN),
            buf(tok, W_IN),
            buf(tok, QW),
            buf(tok, 2 * HEAD),
            buf(tok, 2 * HEAD),
            buf(QW, nt * nz * ROWS),
            buf(QW, C),
            pltpu.SemaphoreType.DMA((SEMS,)),
            pltpu.SemaphoreType.DMA((SEMS,)),
            pltpu.SemaphoreType.DMA((4,)),
        ],
        compiler_params=pltpu.CompilerParams(
            collective_id=0, has_side_effects=True, vmem_limit_bytes=48 * 2**20
        ),
    )(
        resid_in[0],
        attn_in[0],
        seg_fwd[0],
        len_bwd[0],
        out_weight[0],
        stash_held[0],
        out_grad[0],
        evict_slot,
        fetch_slot,
    )
    return tuple(x[None] for x in outs)


def solution(mesh):
    dims = tuple(mesh.shape[a] for a in ("section", "dp", "tensor"))
    placed = (
        P("section", ("dp", "tensor"), None),
        P("section", "dp", "tensor"),
        P("section", "dp", None),
        P("section", "tensor", "dp"),
        P("section", None, "dp", "tensor"),
        P("section", "dp", None),
        P("section", ("dp", "tensor"), None),
        P("section"),
        P("section", "dp"),
    )
    return jax.shard_map(
        functools.partial(body, dims),
        mesh=mesh,
        in_specs=placed,
        out_specs=(
            P("section", ("dp", "tensor"), None),
            P("section", None, "dp", "tensor"),
            P("section", "tensor", "dp"),
            P("section", "dp", "tensor"),
        ),
        check_vma=False,
    )
```

```python
import functools

import jax
import jax.numpy as jnp
from jax import lax
from jax.experimental import pallas as pl
from jax.experimental.pallas import tpu as pltpu
from jax.sharding import PartitionSpec as P

HEAD = 128
ROWS = 8
MESH = pl.DeviceIdType.MESH
F32 = jnp.float32
BF16 = jnp.bfloat16
SEMS = 160


def dot(a, b, ca=1, cb=0):
    return lax.dot_general(a, b, (((ca,), (cb,)), ((), ())), preferred_element_type=F32)


def probabilities(q, k, allowed, heads):
    tok = k.shape[0]
    scores = dot(q, k, 1, 1).reshape(heads, tok, tok) * HEAD ** (-0.5)
    masked = jnp.where(allowed[None], scores, -1e30)
    highest = jnp.max(masked, axis=-1, keepdims=True)
    raised = jnp.where(allowed[None], jnp.exp(masked - highest), 0.0)
    return (raised / jnp.sum(raised, axis=-1, keepdims=True)).reshape(heads * tok, tok)


def stack_heads(x, heads):
    return jnp.concatenate([x[:, h * HEAD : (h + 1) * HEAD] for h in range(heads)], axis=0)


def unstack_heads(x, heads):
    tok = x.shape[0] // heads
    return jnp.concatenate([x[h * tok : (h + 1) * tok] for h in range(heads)], axis=1)


def to_tall(x):
    half = x.shape[1] // 2
    return jnp.concatenate([x[:, :half], x[:, half:]], axis=0)


def to_wide(x):
    return jnp.concatenate([x[:ROWS], x[ROWS:]], axis=1)


class Pool:
    def __init__(self, sems):
        self.sems, self.count = sems, 0

    def new(self):
        assert self.count < SEMS
        self.count += 1
        return self.sems.at[self.count - 1]


class Sends:
    def __init__(self, pool, view, device):
        self.pool, self.view, self.device = pool, view, device
        self.sem = pool.new()

    def send(self, src, dst, device, recv=None):
        copy = pltpu.make_async_remote_copy(
            src_ref=src,
            dst_ref=dst,
            send_sem=self.sem,
            recv_sem=self.pool.new() if recv is None else recv,
            device_id=device,
            device_id_type=MESH,
        )
        copy.start()
        return copy

    def whole(self, recv=None):
        return pltpu.make_async_remote_copy(
            src_ref=self.view,
            dst_ref=self.view,
            send_sem=self.sem,
            recv_sem=self.sem if recv is None else recv,
            device_id=self.device,
            device_id_type=MESH,
        )

    def finish(self):
        self.whole().wait_send()


class Gather:
    def __init__(self, sends, n, me, device, streams, source, target):
        self.sends, self.n, self.me, self.device = sends, n, me, device
        self.streams, self.source, self.target = streams, source, target
        self.moves = {}

    def step(self, r, parts=None):
        for way, part, hops in self.streams:
            if parts is not None and part not in parts:
                continue
            if 1 <= r <= hops:
                self.moves[(way, part, r - 1)].wait_recv()
            if r < hops:
                to = (self.me + way + self.n) % self.n
                self.moves[(way, part, r)] = self.sends.send(
                    self.source(way, part, r), self.target(way, part, r), self.device(to)
                )


class RingSum:
    def __init__(self, sends, me, n, device, slot, parts):
        self.sends, self.me, self.n, self.device = sends, me, n, device
        self.slot, self.parts = slot, parts
        self.moves, self.terms = {}, {}

    def hops(self, side, p):
        return 4 if (p < len(self.parts) // 2) == (side == 0) else 3

    def step(self, r, term, parts=None):
        for p, (lo, count) in enumerate(self.parts):
            if parts is not None and p not in parts:
                continue
            for side, way in enumerate((1, -1)):
                first = 4 - self.hops(side, p)
                if r < first:
                    continue
                rel = 4 if r == 0 else way * (4 - r)
                if rel not in self.terms:
                    self.terms[rel] = term(rel)
                value = self.terms[rel][lo : lo + count]
                here = self.slot(side, r).at[pl.ds(lo, count)]
                there = self.slot(side, r + 1).at[pl.ds(lo, count)]
                if r > first:
                    self.moves[(side, p, r - 1)].wait_recv()
                    value = value + here[...].astype(F32)
                here[...] = value.astype(BF16)
                to = self.device((self.me + way + self.n) % self.n)
                self.moves[(side, p, r)] = self.sends.send(here, there, to)

    def last(self):
        for p in range(len(self.parts)):
            for side in (0, 1):
                self.moves[(side, p, 3)].wait_recv()
        return self.slot(0, 4)[...].astype(F32) + self.slot(1, 4)[...].astype(F32)


NEAR = (0, 1, -1, 2, -2, 3, -3, 4)
FAR = (4, 3, -3, 2, -2, 1, -1, 0)
A_PARTS, O_PARTS, G_PARTS = 2, 2, 4
X_HOPS = 2


def kernel(
    dims,
    resid_hbm,
    attn_in_hbm,
    seg_hbm,
    lens_hbm,
    weight_hbm,
    stash_hbm,
    out_grad_hbm,
    evict,
    fetch,
    lay_out,
    stash_out,
    wgrad_out,
    agrad_out,
    resid,
    attn_in,
    seg,
    lens,
    weight,
    stash,
    out_grad,
    b1s,
    b1r,
    G,
    part,
    zslots,
    A,
    O,
    yslots,
    f5s,
    f5r,
    xs,
    xr,
    attb,
    reto,
    reto_via,
    retq,
    retq_via,
    retr,
    evp_via,
    evp,
    eva_via,
    eva,
    shs,
    shr,
    OT,
    dnat,
    sems,
    local_sems,
):
    n_sec, nz, nt = dims
    ny = nt // 2
    tok = nt * ROWS
    C = weight.shape[1]
    QW = weight.shape[0]
    heads = QW // HEAD
    W_IN = QW + 2 * HEAD

    sec = lax.axis_index("section")
    z = lax.axis_index("dp")
    t = lax.axis_index("tensor")
    xh = t // ny
    y = t % ny
    other_core = {"section": sec + 1 - 2 * (sec % 2)}
    next_chip = {"section": (sec + n_sec // 2) % n_sec}
    xpeer = {"tensor": (1 - xh) * ny + y}
    pair = {"tensor": t + 1 - 2 * (t % 2)}

    def zdev(i):
        return {"dp": i}

    def ydev(i):
        return {"tensor": xh * ny + i}

    def xdev(i):
        return {"dp": i, "tensor": (1 - xh) * ny + y}

    def at_y(rel):
        return (y + rel + ny) % ny

    def at_z(rel):
        return (z + rel + nz) % nz

    barrier = pltpu.get_barrier_semaphore()
    greeted = [zdev(at_z(k)) for k in range(1, nz)]
    greeted += [xpeer]
    greeted += [ydev(at_y(1)), ydev(at_y(-1)), other_core, next_chip]
    for device in greeted:
        pl.semaphore_signal(barrier, inc=1, device_id=device, device_id_type=MESH)

    pairs = [
        (out_grad_hbm, out_grad),
        (stash_hbm, stash),
        (attn_in_hbm, attn_in),
        (seg_hbm, seg),
        (weight_hbm, weight),
        (lens_hbm, lens),
        (resid_hbm, resid),
    ]
    loads = [pltpu.make_async_copy(a, b, local_sems.at[i]) for i, (a, b) in enumerate(pairs)]
    for load in loads:
        load.start()
    loads[0].wait()

    pool = Pool(sems)
    groups = []

    def sends(view, device):
        groups.append(Sends(pool, view, device))
        return groups[-1]

    for d in range(nz):
        b1s[d] = to_tall(out_grad[:, d * C : (d + 1) * C].astype(F32)).astype(BF16)
    b1r[z] = b1s[z]

    pl.semaphore_wait(barrier, len(greeted))

    some_z = zdev(at_z(1))
    some_y = ydev(at_y(1))
    b1 = sends(b1r.at[pl.ds(0, nz - 1)], some_z)
    b1_recv = pool.new()
    for k in (4, 3, -3, 2, -2, 1, -1):
        b1.send(b1s.at[at_z(k)], b1r.at[z], zdev(at_z(k)), b1_recv)

    def permuted(x):
        return [
            jnp.concatenate(
                [x[h * ny * ROWS + b * ROWS : h * ny * ROWS + (b + 1) * ROWS] for h in (0, 1)],
                axis=0,
            )
            for b in range(ny)
        ]

    def natural(x):
        return jnp.concatenate(
            [x[(2 * b + h) * ROWS : (2 * b + h + 1) * ROWS] for h in (0, 1) for b in range(ny)],
            axis=0,
        )

    loads[1].wait()
    slot = fetch[0, 0]
    held = stash[slot]
    for b, rows in enumerate(permuted(held[:, W_IN:].astype(F32))):
        reto[b] = rows.astype(BF16)
    retq[...] = held[:, :W_IN]

    def across_core(src, via):
        return sends(src, other_core).send(src, via, other_core)

    def to_mirror(via, dst):
        return sends(via, next_chip).send(via, dst, next_chip)

    core_o = across_core(reto, reto_via)
    core_q = across_core(retq, retq_via)

    loads[2].wait()
    core_p = across_core(attn_in, evp_via)
    loads[3].wait()
    row_id = lax.broadcasted_iota(jnp.int32, (tok, tok), 0)
    col_id = lax.broadcasted_iota(jnp.int32, (tok, tok), 1)
    seg_cols = jnp.broadcast_to(seg[...].astype(F32), (tok, tok))
    allowed = (seg_cols == jnp.transpose(seg_cols)) & (col_id <= row_id)
    q = stack_heads(attn_in[:, :QW], heads)
    k = attn_in[:, QW : QW + HEAD]
    v = attn_in[:, QW + HEAD : W_IN]
    weights = probabilities(q, k, allowed, heads).astype(BF16)
    att = unstack_heads(dot(weights, v), heads)
    attb[...] = att.astype(BF16)
    core_a = across_core(attb, eva_via)
    for b, rows in enumerate(permuted(att)):
        A[0, b] = rows.astype(BF16)


    def two_way(parts):
        return [
            (way, p, 4 if (p < parts // 2) == (way == 1) else 3)
            for p in range(parts)
            for way in (1, -1)
        ]

    def a_piece(rel, h):
        return A.at[NEAR.index(rel), pl.ds(h * ny // A_PARTS, ny // A_PARTS)]

    def ring_rel(rel):
        return 4 if rel == -4 else rel

    gather_a = Gather(
        sends(A.at[pl.ds(0, nz - 1)], some_z),
        nz,
        z,
        zdev,
        two_way(A_PARTS),
        lambda way, h, r: a_piece(ring_rel(-way * r), h),
        lambda way, h, r: a_piece(ring_rel(-way * (r + 1)), h),
    )

    def o_piece(way, h, r):
        return O.at[at_z(-way * r), pl.ds(h * ny // O_PARTS, ny // O_PARTS)]

    gather_o = Gather(
        sends(O.at[pl.ds(0, nz - 1)], some_z), nz, z, zdev, two_way(O_PARTS), o_piece, o_piece
    )

    sub = nz * ROWS // G_PARTS

    def g_piece(way, h, r):
        return G.at[at_y(-way * r), xh, pl.ds(h * sub, sub)]

    gather_g = Gather(
        sends(G.at[pl.ds(0, ny - 1), 0], some_y), ny, y, ydev, two_way(G_PARTS), g_piece, g_piece
    )

    def other_piece(way, h, r):
        return G.at[at_y(-way * r), 1 - xh]

    gather_other = Gather(
        sends(G.at[pl.ds(0, 2 * X_HOPS), 0], some_y),
        ny,
        y,
        ydev,
        ((1, 0, X_HOPS), (-1, 0, X_HOPS)),
        other_piece,
        other_piece,
    )
    across = [0] + [rel for rel in NEAR if abs(rel) > X_HOPS]
    g_x = sends(G.at[pl.ds(0, len(across)), 0], xpeer)
    g_x_moves = {}

    def send_across(rel):
        ref = G.at[at_y(rel), xh]
        g_x_moves[rel] = g_x.send(ref, ref, xpeer)

    gather_a.step(0)

    def cotangent_piece(group, recv, h, at):
        group.whole(recv).wait_recv()
        for p in range(nz // 2):
            rows = [to_wide(b1r[h * nz + 2 * p + j].astype(F32)) for j in (0, 1)]
            G[y, at, pl.ds(2 * ROWS * p, 2 * ROWS), :] = jnp.concatenate(rows, axis=0).astype(BF16)

    cotangent_piece(b1, b1_recv, 0, xh)
    gather_g.step(0)
    send_across(0)
    gather_a.step(1)

    for load in loads[4:]:
        load.wait()

    Z_SPLIT = ((0, 5, 3), (5, 3, 2))
    z_sums = []
    for lo, count, cut in Z_SPLIT:
        z_sums.append(
            RingSum(
                sends(O.at[pl.ds(0, nz - 1), pl.ds(0, count)], some_z),
                z,
                nz,
                zdev,
                lambda side, r, lo=lo, count=count: zslots.at[side, r, pl.ds(lo, count)],
                ((0, cut), (cut, count - cut)),
            )
        )

    def head_grad_part(rels):
        for rel in rels:
            b = at_y(rel)
            res = dot(G[b].reshape(2 * nz * ROWS, C), weight[...], 1, 1)
            for d in range(nz):
                both = [res[(h * nz + d) * ROWS : (h * nz + d + 1) * ROWS] for h in (0, 1)]
                part[d, NEAR.index(rel)] = jnp.concatenate(both, axis=0).astype(BF16)

    def head_grad_step(i, r):
        lo, count, _ = Z_SPLIT[i]
        z_sums[i].step(r, lambda rel: part[at_z(rel), pl.ds(lo, count)].astype(F32))

    RUNS = nz // 2
    y_sums = [
        RingSum(
            sends(G.at[pl.ds(0, ny - 1), 0], some_y),
            y,
            ny,
            ydev,
            lambda side, r, g=g: yslots.at[g, side, r],
            ((0, RUNS * ROWS), (RUNS * ROWS, RUNS * ROWS)),
        )
        for g in (0, 1)
    ]

    def branch_term(g, rel):
        rows = A[pl.ds(g * RUNS, RUNS), at_y(rel)].reshape(RUNS * 2 * ROWS, QW)
        return dot(rows, weight[...])

    def branch_step(g, r):
        y_sums[g].step(r, lambda rel: branch_term(g, rel))

    f5 = sends(f5r.at[pl.ds(0, nz - 1)], some_z)
    f5_recv = pool.new()
    keep, x_moves = {}, {}

    def branch_x(g):
        total = branch_term(g, 0) + y_sums[g].last()
        halves = [
            jnp.concatenate(
                [total[(2 * j + h) * ROWS : (2 * j + h + 1) * ROWS] for j in range(RUNS)], axis=0
            )
            for h in (0, 1)
        ]
        xs[g] = jnp.where(xh == 0, halves[1], halves[0]).astype(BF16)
        x_moves[g] = sends(xs.at[g], xpeer).send(xs.at[g], xr.at[g], xpeer)
        keep[g] = jnp.where(xh == 0, halves[0], halves[1])

    def branch_end(g):
        x_moves[g].wait_recv()
        total = keep[g] + xr[g].astype(F32)
        for j in reversed(range(RUNS)):
            slot = g * RUNS + j
            rel = NEAR[slot]
            tall = to_tall(total[j * ROWS : (j + 1) * ROWS]).astype(BF16)
            if rel == 0:
                f5r[z] = tall
            else:
                f5s[slot] = tall
                f5.send(f5s.at[slot], f5r.at[z], zdev(at_z(rel)), f5_recv)

    def weight_grad_part(i):
        cols = pl.ds(i * (C // 4), C // 4)
        wgrad_out[:, cols] = dot(
            OT[...], G[:, :, :, cols].reshape(nt * nz * ROWS, C // 4)
        ).astype(BF16)

    def arrange_outputs():
        for b in range(ny):
            x = O[:, b].astype(F32)
            rows = [x[d, h * ROWS : (h + 1) * ROWS] for h in (0, 1) for d in range(nz)]
            block = jnp.concatenate(rows, axis=0)
            width = 2 * nz * ROWS
            OT[:, b * width : (b + 1) * width] = jnp.transpose(block).astype(BF16)

    core_o.wait_recv()
    move_ret_o = to_mirror(reto_via, O.at[z])
    gather_g.step(1)
    g_x_moves[0].wait_recv()
    gather_other.step(0)
    gather_a.step(2)
    head_grad_part((0,))
    branch_step(0, 0)
    gather_g.step(2)
    gather_other.step(1)
    gather_a.step(3)
    head_grad_part((1, -1))
    move_ret_o.wait_recv()
    gather_o.step(0)
    branch_step(0, 1)
    gather_g.step(3)
    send_across(3)
    send_across(-3)
    gather_other.step(2)
    head_grad_part((2, -2))
    head_grad_step(0, 0)
    gather_a.step(4)
    branch_step(1, 0)
    branch_step(0, 2)
    gather_g.step(4)
    send_across(4)
    gather_o.step(1)
    head_grad_step(0, 1)
    branch_step(1, 1)
    g_x_moves[3].wait_recv()
    g_x_moves[-3].wait_recv()
    head_grad_part((3, -3))
    branch_step(0, 3)
    g_x_moves[4].wait_recv()
    head_grad_part((4,))
    head_grad_step(1, 0)
    core_q.wait_recv()
    move_ret_q = to_mirror(retq_via, retr)
    gather_o.step(2)
    head_grad_step(0, 2)
    branch_step(1, 2)
    head_grad_step(1, 1)
    core_p.wait_recv()
    core_a.wait_recv()
    move_ev_p = to_mirror(evp_via, evp)
    move_ev_a = to_mirror(eva_via, eva)
    branch_x(0)
    gather_o.step(3)
    head_grad_step(0, 3)
    branch_step(1, 3)
    head_grad_step(1, 2)
    branch_end(0)
    gather_o.step(4)
    arrange_outputs()
    for i in range(2):
        weight_grad_part(i)
    head_grad_step(1, 3)
    branch_x(1)
    for i in range(2, 4):
        weight_grad_part(i)

    move_ret_q.wait_recv()
    end = jnp.int32(0)
    seg_row = jnp.zeros((tok, tok), jnp.int32)
    seg_col = jnp.zeros((tok, tok), jnp.int32)
    for c in range(lens.shape[1]):
        end = end + lens[0, c]
        seg_row += (row_id >= end).astype(jnp.int32)
        seg_col += (col_id >= end).astype(jnp.int32)
    allowed = (seg_row == seg_col) & (col_id <= row_id)
    q = stack_heads(retr[:, :QW], heads)
    k = retr[:, QW : QW + HEAD]
    v = retr[:, QW + HEAD : W_IN]
    probs = probabilities(q, k, allowed, heads)
    old = natural(O[z].astype(F32).reshape(tok, QW))

    branch_end(1)

    sums = jnp.concatenate([z_sums[0].last(), z_sums[1].last()], axis=0)
    total = part[z].astype(F32) + sums
    for j, rel in enumerate(NEAR):
        for h in (0, 1):
            row = pl.multiple_of((h * ny + at_y(rel)) * ROWS, ROWS)
            dnat[pl.ds(row, ROWS), :] = total[j, h * ROWS : (h + 1) * ROWS]
    d_out = dnat[...].astype(BF16)
    d_heads = stack_heads(d_out, heads)
    grad_v = dot(probs.astype(BF16), d_heads, 0, 0)
    grad_p = dot(d_heads, v, 1, 1)
    inner = jnp.sum(d_heads.astype(F32) * stack_heads(old, heads), axis=-1, keepdims=True)
    grad_s = (probs * (grad_p - inner)).astype(BF16)
    grad_k = dot(grad_s, q, 0, 0) * HEAD ** (-0.5)
    shs[:, :HEAD] = grad_k.astype(BF16)
    shs[:, HEAD:] = grad_v.astype(BF16)
    move_shared = sends(shs, pair).send(shs, shr, pair)
    grad_q = dot(grad_s, k) * HEAD ** (-0.5)
    agrad_out[:, :QW] = unstack_heads(grad_q, heads).astype(BF16)
    move_ev_p.wait_recv()
    move_ev_a.wait_recv()
    for i in range(stash.shape[0]):
        here = evict[0] == i
        stash_out[i, :, :W_IN] = jnp.where(here, evp[...], stash[i, :, :W_IN])
        stash_out[i, :, W_IN:] = jnp.where(here, eva[...], stash[i, :, W_IN:])

    move_shared.wait_recv()
    agrad_out[:, QW:] = (shs[...].astype(F32) + shr[...].astype(F32)).astype(BF16)

    f5.whole(f5_recv).wait_recv()
    for d in range(nz):
        cols = slice(d * C, (d + 1) * C)
        summed = to_wide(f5r[d].astype(F32))
        lay_out[:, cols] = (resid[:, cols].astype(F32) + summed).astype(BF16)

    for group in groups:
        group.finish()


def body(
    dims,
    resid_in,
    attn_in,
    seg_fwd,
    out_weight,
    stash_held,
    len_bwd,
    out_grad,
    evict_slot,
    fetch_slot,
):
    n_sec, nz, nt = dims
    ny = nt // 2
    tok = nt * ROWS
    QW, C = out_weight.shape[1:]
    D = resid_in.shape[-1]
    W_IN = QW + 2 * HEAD
    slots, width = stash_held.shape[1], stash_held.shape[-1]
    vmem, smem, hbm = (
        pl.BlockSpec(memory_space=s) for s in (pltpu.VMEM, pltpu.SMEM, pltpu.HBM)
    )

    def buf(*shape):
        return pltpu.VMEM(shape, BF16)

    outs = pl.pallas_call(
        functools.partial(kernel, dims),
        out_shape=(
            jax.ShapeDtypeStruct((ROWS, D), BF16),
            jax.ShapeDtypeStruct((slots, tok, width), BF16),
            jax.ShapeDtypeStruct((QW, C), BF16),
            jax.ShapeDtypeStruct((tok, W_IN), BF16),
        ),
        in_specs=[hbm] * 7 + [smem] * 2,
        out_specs=(vmem,) * 4,
        scratch_shapes=[
            buf(ROWS, D),
            buf(tok, W_IN),
            pltpu.VMEM((1, tok), jnp.int32),
            pltpu.SMEM(len_bwd.shape[1:], jnp.int32),
            buf(QW, C),
            buf(slots, tok, width),
            buf(ROWS, D),
            buf(nz, 2 * ROWS, C // 2),
            buf(2 * nz, 2 * ROWS, C // 2),
            buf(ny, 2, nz * ROWS, C),
            buf(nz, ny, 2 * ROWS, QW),
            buf(2, nz // 2 + 1, ny, 2 * ROWS, QW),
            buf(nz, ny, 2 * ROWS, QW),
            buf(nz, ny, 2 * ROWS, QW),
            buf(2, 2, ny // 2 + 1, nz * ROWS, C),
            buf(nz, 2 * ROWS, C // 2),
            buf(nz, 2 * ROWS, C // 2),
            buf(2, nz // 2 * ROWS, C),
            buf(2, nz // 2 * ROWS, C),
            buf(tok, QW),
            buf(ny, 2 * ROWS, QW),
            buf(ny, 2 * ROWS, QW),
            buf(tok, W_IN),
            buf(tok, W_IN),
            buf(tok, W_IN),
            buf(tok, W_IN),
            buf(tok, W_IN),
            buf(tok, QW),
            buf(tok, QW),
            buf(tok, 2 * HEAD),
            buf(tok, 2 * HEAD),
            buf(QW, nt * nz * ROWS),
            pltpu.VMEM((tok, QW), F32),
            pltpu.SemaphoreType.DMA((SEMS,)),
            pltpu.SemaphoreType.DMA((7,)),
        ],
        compiler_params=pltpu.CompilerParams(
            collective_id=0, has_side_effects=True, vmem_limit_bytes=48 * 2**20
        ),
    )(
        *(
            pltpu.with_memory_space_constraint(x, pltpu.HBM) if x.size > 1 else x
            for x in (
                resid_in[0],
                attn_in[0],
                seg_fwd[0],
                len_bwd[0],
                out_weight[0],
                stash_held[0],
                out_grad[0],
                evict_slot,
                fetch_slot,
            )
        )
    )
    return tuple(x[None] for x in outs)


def solution(mesh):
    dims = tuple(mesh.shape[a] for a in ("section", "dp", "tensor"))
    placed = (
        P("section", ("dp", "tensor"), None),
        P("section", "dp", "tensor"),
        P("section", "dp", None),
        P("section", "tensor", "dp"),
        P("section", None, "dp", "tensor"),
        P("section", "dp", None),
        P("section", ("dp", "tensor"), None),
        P("section"),
        P("section", "dp"),
    )
    return jax.shard_map(
        functools.partial(body, dims),
        mesh=mesh,
        in_specs=placed,
        out_specs=(
            P("section", ("dp", "tensor"), None),
            P("section", None, "dp", "tensor"),
            P("section", "tensor", "dp"),
            P("section", "dp", "tensor"),
        ),
        check_vma=False,
    )
```

```python
import functools

import jax
import jax.numpy as jnp
from jax import lax
from jax.experimental import pallas as pl
from jax.experimental.pallas import tpu as pltpu
from jax.sharding import PartitionSpec as P

HEAD = 128
ROWS = 8
MESH = pl.DeviceIdType.MESH
F32 = jnp.float32
BF16 = jnp.bfloat16
SEMS = 160


def dot(a, b, ca=1, cb=0):
    return lax.dot_general(a, b, (((ca,), (cb,)), ((), ())), preferred_element_type=F32)


def probabilities(q, k, allowed, heads):
    tok = k.shape[0]
    scores = dot(q, k, 1, 1).reshape(heads, tok, tok) * HEAD ** (-0.5)
    masked = jnp.where(allowed[None], scores, -1e30)
    highest = jnp.max(masked, axis=-1, keepdims=True)
    raised = jnp.where(allowed[None], jnp.exp(masked - highest), 0.0)
    return (raised / jnp.sum(raised, axis=-1, keepdims=True)).reshape(heads * tok, tok)


def stack_heads(x, heads):
    return jnp.concatenate([x[:, h * HEAD : (h + 1) * HEAD] for h in range(heads)], axis=0)


def unstack_heads(x, heads):
    tok = x.shape[0] // heads
    return jnp.concatenate([x[h * tok : (h + 1) * tok] for h in range(heads)], axis=1)


def to_tall(x):
    half = x.shape[1] // 2
    return jnp.concatenate([x[:, :half], x[:, half:]], axis=0)


def to_wide(x):
    return jnp.concatenate([x[:ROWS], x[ROWS:]], axis=1)


class Pool:
    def __init__(self, sems):
        self.sems, self.count = sems, 0

    def new(self):
        assert self.count < SEMS
        self.count += 1
        return self.sems.at[self.count - 1]


class Sends:
    def __init__(self, pool, view, device):
        self.pool, self.view, self.device = pool, view, device
        self.sem = pool.new()

    def send(self, src, dst, device, recv=None):
        copy = pltpu.make_async_remote_copy(
            src_ref=src,
            dst_ref=dst,
            send_sem=self.sem,
            recv_sem=self.pool.new() if recv is None else recv,
            device_id=device,
            device_id_type=MESH,
        )
        copy.start()
        return copy

    def whole(self, recv=None):
        return pltpu.make_async_remote_copy(
            src_ref=self.view,
            dst_ref=self.view,
            send_sem=self.sem,
            recv_sem=self.sem if recv is None else recv,
            device_id=self.device,
            device_id_type=MESH,
        )

    def finish(self):
        self.whole().wait_send()


class Gather:
    def __init__(self, sends, n, me, device, streams, source, target):
        self.sends, self.n, self.me, self.device = sends, n, me, device
        self.streams, self.source, self.target = streams, source, target
        self.moves = {}

    def step(self, r, parts=None):
        for way, part, hops in self.streams:
            if parts is not None and part not in parts:
                continue
            if 1 <= r <= hops:
                self.moves[(way, part, r - 1)].wait_recv()
            if r < hops:
                to = (self.me + way + self.n) % self.n
                self.moves[(way, part, r)] = self.sends.send(
                    self.source(way, part, r), self.target(way, part, r), self.device(to)
                )


class RingSum:
    def __init__(self, sends, me, n, device, slot, parts):
        self.sends, self.me, self.n, self.device = sends, me, n, device
        self.slot, self.parts = slot, parts
        self.moves, self.terms = {}, {}

    def hops(self, side, p):
        return 4 if (p < len(self.parts) // 2) == (side == 0) else 3

    def step(self, r, term, parts=None):
        for p, (lo, count) in enumerate(self.parts):
            if parts is not None and p not in parts:
                continue
            for side, way in enumerate((1, -1)):
                first = 4 - self.hops(side, p)
                if r < first:
                    continue
                rel = 4 if r == 0 else way * (4 - r)
                if rel not in self.terms:
                    self.terms[rel] = term(rel)
                value = self.terms[rel][lo : lo + count]
                here = self.slot(side, r).at[pl.ds(lo, count)]
                there = self.slot(side, r + 1).at[pl.ds(lo, count)]
                if r > first:
                    self.moves[(side, p, r - 1)].wait_recv()
                    value = value + here[...].astype(F32)
                here[...] = value.astype(BF16)
                to = self.device((self.me + way + self.n) % self.n)
                self.moves[(side, p, r)] = self.sends.send(here, there, to)

    def last(self):
        for p in range(len(self.parts)):
            for side in (0, 1):
                self.moves[(side, p, 3)].wait_recv()
        return self.slot(0, 4)[...].astype(F32) + self.slot(1, 4)[...].astype(F32)


NEAR = (0, 1, -1, 2, -2, 3, -3, 4)
FAR = (4, 3, -3, 2, -2, 1, -1, 0)
A_PARTS, O_PARTS, G_PARTS = 2, 2, 4
X_HOPS = 1


def kernel(
    dims,
    resid_hbm,
    attn_in_hbm,
    seg_hbm,
    lens_hbm,
    weight_hbm,
    stash_hbm,
    out_grad_hbm,
    evict,
    fetch,
    lay_out,
    stash_out,
    wgrad_out,
    agrad_out,
    resid,
    attn_in,
    seg,
    lens,
    weight,
    stash,
    out_grad,
    b1s,
    b1r,
    G,
    part,
    zslots,
    A,
    O,
    yslots,
    f5s,
    f5r,
    xs,
    xr,
    attb,
    reto,
    reto_via,
    retq,
    retq_via,
    retr,
    evp_via,
    evp,
    eva_via,
    eva,
    shs,
    shr,
    OT,
    dnat,
    sems,
    local_sems,
):
    n_sec, nz, nt = dims
    ny = nt // 2
    tok = nt * ROWS
    C = weight.shape[1]
    QW = weight.shape[0]
    heads = QW // HEAD
    W_IN = QW + 2 * HEAD

    sec = lax.axis_index("section")
    z = lax.axis_index("dp")
    t = lax.axis_index("tensor")
    xh = t // ny
    y = t % ny
    other_core = {"section": sec + 1 - 2 * (sec % 2)}
    next_chip = {"section": (sec + n_sec // 2) % n_sec}
    xpeer = {"tensor": (1 - xh) * ny + y}
    pair = {"tensor": t + 1 - 2 * (t % 2)}

    def zdev(i):
        return {"dp": i}

    def ydev(i):
        return {"tensor": xh * ny + i}

    def xdev(i):
        return {"dp": i, "tensor": (1 - xh) * ny + y}

    def at_y(rel):
        return (y + rel + ny) % ny

    def at_z(rel):
        return (z + rel + nz) % nz

    barrier = pltpu.get_barrier_semaphore()
    greeted = [zdev(at_z(k)) for k in range(1, nz)]
    greeted += [xpeer]
    greeted += [ydev(at_y(1)), ydev(at_y(-1)), other_core, next_chip]
    for device in greeted:
        pl.semaphore_signal(barrier, inc=1, device_id=device, device_id_type=MESH)

    pairs = [
        (out_grad_hbm, out_grad),
        (stash_hbm, stash),
        (attn_in_hbm, attn_in),
        (seg_hbm, seg),
        (weight_hbm, weight),
        (lens_hbm, lens),
        (resid_hbm, resid),
    ]
    loads = [pltpu.make_async_copy(a, b, local_sems.at[i]) for i, (a, b) in enumerate(pairs)]
    for load in loads:
        load.start()
    loads[0].wait()

    pool = Pool(sems)
    groups = []

    def sends(view, device):
        groups.append(Sends(pool, view, device))
        return groups[-1]

    for d in range(nz):
        b1s[d] = to_tall(out_grad[:, d * C : (d + 1) * C].astype(F32)).astype(BF16)
    b1r[z] = b1s[z]

    pl.semaphore_wait(barrier, len(greeted))

    some_z = zdev(at_z(1))
    some_y = ydev(at_y(1))
    b1 = sends(b1r.at[pl.ds(0, nz - 1)], some_z)
    b1_recv = pool.new()
    for k in (4, 3, -3, 2, -2, 1, -1):
        b1.send(b1s.at[at_z(k)], b1r.at[z], zdev(at_z(k)), b1_recv)

    def permuted(x):
        return [
            jnp.concatenate(
                [x[h * ny * ROWS + b * ROWS : h * ny * ROWS + (b + 1) * ROWS] for h in (0, 1)],
                axis=0,
            )
            for b in range(ny)
        ]

    def natural(x):
        return jnp.concatenate(
            [x[(2 * b + h) * ROWS : (2 * b + h + 1) * ROWS] for h in (0, 1) for b in range(ny)],
            axis=0,
        )

    loads[1].wait()
    slot = fetch[0, 0]
    held = stash[slot]
    for b, rows in enumerate(permuted(held[:, W_IN:].astype(F32))):
        reto[b] = rows.astype(BF16)
    retq[...] = held[:, :W_IN]

    def across_core(src, via):
        return sends(src, other_core).send(src, via, other_core)

    def to_mirror(via, dst):
        return sends(via, next_chip).send(via, dst, next_chip)

    core_o = across_core(reto, reto_via)
    core_q = across_core(retq, retq_via)

    loads[2].wait()
    core_p = across_core(attn_in, evp_via)
    loads[3].wait()
    row_id = lax.broadcasted_iota(jnp.int32, (tok, tok), 0)
    col_id = lax.broadcasted_iota(jnp.int32, (tok, tok), 1)
    seg_cols = jnp.broadcast_to(seg[...].astype(F32), (tok, tok))
    allowed = (seg_cols == jnp.transpose(seg_cols)) & (col_id <= row_id)
    q = stack_heads(attn_in[:, :QW], heads)
    k = attn_in[:, QW : QW + HEAD]
    v = attn_in[:, QW + HEAD : W_IN]
    weights = probabilities(q, k, allowed, heads).astype(BF16)
    att = unstack_heads(dot(weights, v), heads)
    attb[...] = att.astype(BF16)
    core_a = across_core(attb, eva_via)
    for b, rows in enumerate(permuted(att)):
        A[0, b] = rows.astype(BF16)


    def two_way(parts):
        return [
            (way, p, 4 if (p < parts // 2) == (way == 1) else 3)
            for p in range(parts)
            for way in (1, -1)
        ]

    def a_piece(rel, h):
        return A.at[NEAR.index(rel), pl.ds(h * ny // A_PARTS, ny // A_PARTS)]

    def ring_rel(rel):
        return 4 if rel == -4 else rel

    gather_a = Gather(
        sends(A.at[pl.ds(0, nz - 1)], some_z),
        nz,
        z,
        zdev,
        two_way(A_PARTS),
        lambda way, h, r: a_piece(ring_rel(-way * r), h),
        lambda way, h, r: a_piece(ring_rel(-way * (r + 1)), h),
    )

    def o_piece(way, h, r):
        return O.at[at_z(-way * r), pl.ds(h * ny // O_PARTS, ny // O_PARTS)]

    gather_o = Gather(
        sends(O.at[pl.ds(0, nz - 1)], some_z), nz, z, zdev, two_way(O_PARTS), o_piece, o_piece
    )

    sub = nz * ROWS // G_PARTS

    def g_piece(way, h, r):
        return G.at[at_y(-way * r), xh, pl.ds(h * sub, sub)]

    gather_g = Gather(
        sends(G.at[pl.ds(0, ny - 1), 0], some_y), ny, y, ydev, two_way(G_PARTS), g_piece, g_piece
    )

    def other_piece(way, h, r):
        return G.at[at_y(-way * r), 1 - xh]

    gather_other = Gather(
        sends(G.at[pl.ds(0, 2 * X_HOPS), 0], some_y),
        ny,
        y,
        ydev,
        ((1, 0, X_HOPS), (-1, 0, X_HOPS)),
        other_piece,
        other_piece,
    )
    across = [0] + [rel for rel in NEAR if abs(rel) > X_HOPS]
    g_x = sends(G.at[pl.ds(0, len(across)), 0], xpeer)
    g_x_moves = {}

    def send_across(rel):
        ref = G.at[at_y(rel), xh]
        g_x_moves[rel] = g_x.send(ref, ref, xpeer)

    gather_a.step(0)

    def cotangent_piece(group, recv, h, at):
        group.whole(recv).wait_recv()
        for p in range(nz // 2):
            rows = [to_wide(b1r[h * nz + 2 * p + j].astype(F32)) for j in (0, 1)]
            G[y, at, pl.ds(2 * ROWS * p, 2 * ROWS), :] = jnp.concatenate(rows, axis=0).astype(BF16)

    cotangent_piece(b1, b1_recv, 0, xh)
    gather_g.step(0)
    send_across(0)
    gather_a.step(1)

    for load in loads[4:]:
        load.wait()

    Z_SPLIT = ((0, 5, 3), (5, 3, 2))
    z_sums = []
    for lo, count, cut in Z_SPLIT:
        z_sums.append(
            RingSum(
                sends(O.at[pl.ds(0, nz - 1), pl.ds(0, count)], some_z),
                z,
                nz,
                zdev,
                lambda side, r, lo=lo, count=count: zslots.at[side, r, pl.ds(lo, count)],
                ((0, cut), (cut, count - cut)),
            )
        )

    def head_grad_part(rels):
        for rel in rels:
            b = at_y(rel)
            res = dot(G[b].reshape(2 * nz * ROWS, C), weight[...], 1, 1)
            for d in range(nz):
                both = [res[(h * nz + d) * ROWS : (h * nz + d + 1) * ROWS] for h in (0, 1)]
                part[d, NEAR.index(rel)] = jnp.concatenate(both, axis=0).astype(BF16)

    def head_grad_step(i, r):
        lo, count, _ = Z_SPLIT[i]
        z_sums[i].step(r, lambda rel: part[at_z(rel), pl.ds(lo, count)].astype(F32))

    RUNS = nz // 2
    y_sums = [
        RingSum(
            sends(G.at[pl.ds(0, ny - 1), 0], some_y),
            y,
            ny,
            ydev,
            lambda side, r, g=g: yslots.at[g, side, r],
            ((0, RUNS * ROWS), (RUNS * ROWS, RUNS * ROWS)),
        )
        for g in (0, 1)
    ]

    def branch_term(g, rel):
        rows = A[pl.ds(g * RUNS, RUNS), at_y(rel)].reshape(RUNS * 2 * ROWS, QW)
        return dot(rows, weight[...])

    def branch_step(g, r):
        y_sums[g].step(r, lambda rel: branch_term(g, rel))

    f5 = sends(f5r.at[pl.ds(0, nz - 1)], some_z)
    f5_recv = pool.new()
    keep, x_moves = {}, {}

    def branch_x(g):
        total = branch_term(g, 0) + y_sums[g].last()
        halves = [
            jnp.concatenate(
                [total[(2 * j + h) * ROWS : (2 * j + h + 1) * ROWS] for j in range(RUNS)], axis=0
            )
            for h in (0, 1)
        ]
        xs[g] = jnp.where(xh == 0, halves[1], halves[0]).astype(BF16)
        x_moves[g] = sends(xs.at[g], xpeer).send(xs.at[g], xr.at[g], xpeer)
        keep[g] = jnp.where(xh == 0, halves[0], halves[1])

    def branch_end(g):
        x_moves[g].wait_recv()
        total = keep[g] + xr[g].astype(F32)
        for j in reversed(range(RUNS)):
            slot = g * RUNS + j
            rel = NEAR[slot]
            tall = to_tall(total[j * ROWS : (j + 1) * ROWS]).astype(BF16)
            if rel == 0:
                f5r[z] = tall
            else:
                f5s[slot] = tall
                f5.send(f5s.at[slot], f5r.at[z], zdev(at_z(rel)), f5_recv)

    def weight_grad_part(i):
        cols = pl.ds(i * (C // 4), C // 4)
        wgrad_out[:, cols] = dot(
            OT[...], G[:, :, :, cols].reshape(nt * nz * ROWS, C // 4)
        ).astype(BF16)

    def arrange_outputs():
        for b in range(ny):
            x = O[:, b].astype(F32)
            rows = [x[d, h * ROWS : (h + 1) * ROWS] for h in (0, 1) for d in range(nz)]
            block = jnp.concatenate(rows, axis=0)
            width = 2 * nz * ROWS
            OT[:, b * width : (b + 1) * width] = jnp.transpose(block).astype(BF16)

    gather_g.step(1)
    g_x_moves[0].wait_recv()
    gather_other.step(0)
    core_o.wait_recv()
    move_ret_o = to_mirror(reto_via, O.at[z])
    gather_a.step(2)
    head_grad_part((0,))
    branch_step(0, 0)
    gather_g.step(2)
    send_across(2)
    send_across(-2)
    gather_other.step(1)
    gather_a.step(3)
    head_grad_part((1, -1))
    branch_step(0, 1)
    gather_g.step(3)
    send_across(3)
    send_across(-3)
    move_ret_o.wait_recv()
    gather_o.step(0)
    g_x_moves[2].wait_recv()
    g_x_moves[-2].wait_recv()
    head_grad_part((2, -2))
    head_grad_step(0, 0)
    gather_a.step(4)
    branch_step(1, 0)
    branch_step(0, 2)
    gather_g.step(4)
    send_across(4)
    gather_o.step(1)
    head_grad_step(0, 1)
    branch_step(1, 1)
    g_x_moves[3].wait_recv()
    g_x_moves[-3].wait_recv()
    head_grad_part((3, -3))
    branch_step(0, 3)
    g_x_moves[4].wait_recv()
    head_grad_part((4,))
    head_grad_step(1, 0)
    core_q.wait_recv()
    move_ret_q = to_mirror(retq_via, retr)
    gather_o.step(2)
    head_grad_step(0, 2)
    branch_step(1, 2)
    head_grad_step(1, 1)
    core_p.wait_recv()
    core_a.wait_recv()
    move_ev_p = to_mirror(evp_via, evp)
    move_ev_a = to_mirror(eva_via, eva)
    branch_x(0)
    gather_o.step(3)
    head_grad_step(0, 3)
    branch_step(1, 3)
    head_grad_step(1, 2)
    branch_end(0)
    gather_o.step(4)
    arrange_outputs()
    head_grad_step(1, 3)
    branch_x(1)

    move_ret_q.wait_recv()
    end = jnp.int32(0)
    seg_row = jnp.zeros((tok, tok), jnp.int32)
    seg_col = jnp.zeros((tok, tok), jnp.int32)
    for c in range(lens.shape[1]):
        end = end + lens[0, c]
        seg_row += (row_id >= end).astype(jnp.int32)
        seg_col += (col_id >= end).astype(jnp.int32)
    allowed = (seg_row == seg_col) & (col_id <= row_id)
    q = stack_heads(retr[:, :QW], heads)
    k = retr[:, QW : QW + HEAD]
    v = retr[:, QW + HEAD : W_IN]
    probs = probabilities(q, k, allowed, heads)
    old = natural(O[z].astype(F32).reshape(tok, QW))

    branch_end(1)

    sums = jnp.concatenate([z_sums[0].last(), z_sums[1].last()], axis=0)
    total = part[z].astype(F32) + sums
    for j, rel in enumerate(NEAR):
        for h in (0, 1):
            row = pl.multiple_of((h * ny + at_y(rel)) * ROWS, ROWS)
            dnat[pl.ds(row, ROWS), :] = total[j, h * ROWS : (h + 1) * ROWS]
    d_out = dnat[...].astype(BF16)
    d_heads = stack_heads(d_out, heads)
    grad_v = dot(probs.astype(BF16), d_heads, 0, 0)
    grad_p = dot(d_heads, v, 1, 1)
    inner = jnp.sum(d_heads.astype(F32) * stack_heads(old, heads), axis=-1, keepdims=True)
    grad_s = (probs * (grad_p - inner)).astype(BF16)
    grad_k = dot(grad_s, q, 0, 0) * HEAD ** (-0.5)
    shs[:, :HEAD] = grad_k.astype(BF16)
    shs[:, HEAD:] = grad_v.astype(BF16)
    move_shared = sends(shs, pair).send(shs, shr, pair)
    grad_q = dot(grad_s, k) * HEAD ** (-0.5)
    agrad_out[:, :QW] = unstack_heads(grad_q, heads).astype(BF16)
    for i in range(4):
        weight_grad_part(i)
    move_ev_p.wait_recv()
    move_ev_a.wait_recv()
    for i in range(stash.shape[0]):
        here = evict[0] == i
        stash_out[i, :, :W_IN] = jnp.where(here, evp[...], stash[i, :, :W_IN])
        stash_out[i, :, W_IN:] = jnp.where(here, eva[...], stash[i, :, W_IN:])

    move_shared.wait_recv()
    agrad_out[:, QW:] = (shs[...].astype(F32) + shr[...].astype(F32)).astype(BF16)

    f5.whole(f5_recv).wait_recv()
    for d in range(nz):
        cols = slice(d * C, (d + 1) * C)
        summed = to_wide(f5r[d].astype(F32))
        lay_out[:, cols] = (resid[:, cols].astype(F32) + summed).astype(BF16)

    for group in groups:
        group.finish()


def body(
    dims,
    resid_in,
    attn_in,
    seg_fwd,
    out_weight,
    stash_held,
    len_bwd,
    out_grad,
    evict_slot,
    fetch_slot,
):
    n_sec, nz, nt = dims
    ny = nt // 2
    tok = nt * ROWS
    QW, C = out_weight.shape[1:]
    D = resid_in.shape[-1]
    W_IN = QW + 2 * HEAD
    slots, width = stash_held.shape[1], stash_held.shape[-1]
    vmem, smem, hbm = (
        pl.BlockSpec(memory_space=s) for s in (pltpu.VMEM, pltpu.SMEM, pltpu.HBM)
    )

    def buf(*shape):
        return pltpu.VMEM(shape, BF16)

    outs = pl.pallas_call(
        functools.partial(kernel, dims),
        out_shape=(
            jax.ShapeDtypeStruct((ROWS, D), BF16),
            jax.ShapeDtypeStruct((slots, tok, width), BF16),
            jax.ShapeDtypeStruct((QW, C), BF16),
            jax.ShapeDtypeStruct((tok, W_IN), BF16),
        ),
        in_specs=[hbm] * 7 + [smem] * 2,
        out_specs=(vmem,) * 4,
        scratch_shapes=[
            buf(ROWS, D),
            buf(tok, W_IN),
            pltpu.VMEM((1, tok), jnp.int32),
            pltpu.SMEM(len_bwd.shape[1:], jnp.int32),
            buf(QW, C),
            buf(slots, tok, width),
            buf(ROWS, D),
            buf(nz, 2 * ROWS, C // 2),
            buf(2 * nz, 2 * ROWS, C // 2),
            buf(ny, 2, nz * ROWS, C),
            buf(nz, ny, 2 * ROWS, QW),
            buf(2, nz // 2 + 1, ny, 2 * ROWS, QW),
            buf(nz, ny, 2 * ROWS, QW),
            buf(nz, ny, 2 * ROWS, QW),
            buf(2, 2, ny // 2 + 1, nz * ROWS, C),
            buf(nz, 2 * ROWS, C // 2),
            buf(nz, 2 * ROWS, C // 2),
            buf(2, nz // 2 * ROWS, C),
            buf(2, nz // 2 * ROWS, C),
            buf(tok, QW),
            buf(ny, 2 * ROWS, QW),
            buf(ny, 2 * ROWS, QW),
            buf(tok, W_IN),
            buf(tok, W_IN),
            buf(tok, W_IN),
            buf(tok, W_IN),
            buf(tok, W_IN),
            buf(tok, QW),
            buf(tok, QW),
            buf(tok, 2 * HEAD),
            buf(tok, 2 * HEAD),
            buf(QW, nt * nz * ROWS),
            pltpu.VMEM((tok, QW), F32),
            pltpu.SemaphoreType.DMA((SEMS,)),
            pltpu.SemaphoreType.DMA((7,)),
        ],
        compiler_params=pltpu.CompilerParams(
            collective_id=0, has_side_effects=True, vmem_limit_bytes=48 * 2**20
        ),
    )(
        *(
            pltpu.with_memory_space_constraint(x, pltpu.HBM) if x.size > 1 else x
            for x in (
                resid_in[0],
                attn_in[0],
                seg_fwd[0],
                len_bwd[0],
                out_weight[0],
                stash_held[0],
                out_grad[0],
                evict_slot,
                fetch_slot,
            )
        )
    )
    return tuple(x[None] for x in outs)


def solution(mesh):
    dims = tuple(mesh.shape[a] for a in ("section", "dp", "tensor"))
    placed = (
        P("section", ("dp", "tensor"), None),
        P("section", "dp", "tensor"),
        P("section", "dp", None),
        P("section", "tensor", "dp"),
        P("section", None, "dp", "tensor"),
        P("section", "dp", None),
        P("section", ("dp", "tensor"), None),
        P("section"),
        P("section", "dp"),
    )
    return jax.shard_map(
        functools.partial(body, dims),
        mesh=mesh,
        in_specs=placed,
        out_specs=(
            P("section", ("dp", "tensor"), None),
            P("section", None, "dp", "tensor"),
            P("section", "tensor", "dp"),
            P("section", "dp", "tensor"),
        ),
        check_vma=False,
    )
```

```python
import functools

import jax
import jax.numpy as jnp
from jax import lax
from jax.experimental import pallas as pl
from jax.experimental.pallas import tpu as pltpu
from jax.sharding import PartitionSpec as P

HEAD = 128
ROWS = 8
MESH = pl.DeviceIdType.MESH
F32 = jnp.float32
BF16 = jnp.bfloat16
SEMS = 160


def dot(a, b, ca=1, cb=0):
    return lax.dot_general(a, b, (((ca,), (cb,)), ((), ())), preferred_element_type=F32)


def probabilities(q, k, allowed, heads):
    tok = k.shape[0]
    scores = dot(q, k, 1, 1).reshape(heads, tok, tok) * HEAD ** (-0.5)
    masked = jnp.where(allowed[None], scores, -1e30)
    highest = jnp.max(masked, axis=-1, keepdims=True)
    raised = jnp.where(allowed[None], jnp.exp(masked - highest), 0.0)
    return (raised / jnp.sum(raised, axis=-1, keepdims=True)).reshape(heads * tok, tok)


def stack_heads(x, heads):
    return jnp.concatenate([x[:, h * HEAD : (h + 1) * HEAD] for h in range(heads)], axis=0)


def unstack_heads(x, heads):
    tok = x.shape[0] // heads
    return jnp.concatenate([x[h * tok : (h + 1) * tok] for h in range(heads)], axis=1)


def to_tall(x):
    half = x.shape[1] // 2
    return jnp.concatenate([x[:, :half], x[:, half:]], axis=0)


def to_wide(x):
    return jnp.concatenate([x[:ROWS], x[ROWS:]], axis=1)


class Pool:
    def __init__(self, sems):
        self.sems, self.count = sems, 0

    def new(self):
        assert self.count < SEMS
        self.count += 1
        return self.sems.at[self.count - 1]


class Sends:
    def __init__(self, pool, view, device):
        self.pool, self.view, self.device = pool, view, device
        self.sem = pool.new()

    def send(self, src, dst, device, recv=None):
        copy = pltpu.make_async_remote_copy(
            src_ref=src,
            dst_ref=dst,
            send_sem=self.sem,
            recv_sem=self.pool.new() if recv is None else recv,
            device_id=device,
            device_id_type=MESH,
        )
        copy.start()
        return copy

    def whole(self, recv=None):
        return pltpu.make_async_remote_copy(
            src_ref=self.view,
            dst_ref=self.view,
            send_sem=self.sem,
            recv_sem=self.sem if recv is None else recv,
            device_id=self.device,
            device_id_type=MESH,
        )

    def finish(self):
        self.whole().wait_send()


class Gather:
    def __init__(self, sends, n, me, device, streams, source, target):
        self.sends, self.n, self.me, self.device = sends, n, me, device
        self.streams, self.source, self.target = streams, source, target
        self.moves = {}

    def step(self, r, parts=None):
        for way, part, hops in self.streams:
            if parts is not None and part not in parts:
                continue
            if 1 <= r <= hops:
                self.moves[(way, part, r - 1)].wait_recv()
            if r < hops:
                to = (self.me + way + self.n) % self.n
                self.moves[(way, part, r)] = self.sends.send(
                    self.source(way, part, r), self.target(way, part, r), self.device(to)
                )


class RingSum:
    def __init__(self, sends, me, n, device, slot, parts):
        self.sends, self.me, self.n, self.device = sends, me, n, device
        self.slot, self.parts = slot, parts
        self.moves, self.terms = {}, {}

    def hops(self, side, p):
        return 4 if (p < len(self.parts) // 2) == (side == 0) else 3

    def step(self, r, term, parts=None):
        for p, (lo, count) in enumerate(self.parts):
            if parts is not None and p not in parts:
                continue
            for side, way in enumerate((1, -1)):
                first = 4 - self.hops(side, p)
                if r < first:
                    continue
                rel = 4 if r == 0 else way * (4 - r)
                if rel not in self.terms:
                    self.terms[rel] = term(rel)
                value = self.terms[rel][lo : lo + count]
                here = self.slot(side, r).at[pl.ds(lo, count)]
                there = self.slot(side, r + 1).at[pl.ds(lo, count)]
                if r > first:
                    self.moves[(side, p, r - 1)].wait_recv()
                    value = value + here[...].astype(F32)
                here[...] = value.astype(BF16)
                to = self.device((self.me + way + self.n) % self.n)
                self.moves[(side, p, r)] = self.sends.send(here, there, to)

    def last(self):
        for p in range(len(self.parts)):
            for side in (0, 1):
                self.moves[(side, p, 3)].wait_recv()
        return self.slot(0, 4)[...].astype(F32) + self.slot(1, 4)[...].astype(F32)


NEAR = (0, 1, -1, 2, -2, 3, -3, 4)
FAR = (4, 3, -3, 2, -2, 1, -1, 0)
A_PARTS, O_PARTS, G_PARTS = 2, 2, 4
X_HOPS = 1


def kernel(
    dims,
    resid_hbm,
    attn_in_hbm,
    seg_hbm,
    lens_hbm,
    weight_hbm,
    stash_hbm,
    out_grad_hbm,
    evict,
    fetch,
    lay_out,
    stash_out,
    wgrad_out,
    agrad_out,
    resid,
    attn_in,
    seg,
    lens,
    weight,
    stash,
    out_grad,
    b1s,
    b1r,
    G,
    part,
    zslots,
    A,
    O,
    yslots,
    f5s,
    f5r,
    xs,
    xr,
    attb,
    reto,
    reto_via,
    retq,
    retq_via,
    retr,
    evp_via,
    evp,
    eva_via,
    eva,
    shs,
    shr,
    OT,
    dnat,
    sems,
    local_sems,
):
    n_sec, nz, nt = dims
    ny = nt // 2
    tok = nt * ROWS
    C = weight.shape[1]
    QW = weight.shape[0]
    heads = QW // HEAD
    W_IN = QW + 2 * HEAD

    sec = lax.axis_index("section")
    z = lax.axis_index("dp")
    t = lax.axis_index("tensor")
    xh = t // ny
    y = t % ny
    other_core = {"section": sec + 1 - 2 * (sec % 2)}
    next_chip = {"section": (sec + n_sec // 2) % n_sec}
    xpeer = {"tensor": (1 - xh) * ny + y}
    pair = {"tensor": t + 1 - 2 * (t % 2)}

    def zdev(i):
        return {"dp": i}

    def ydev(i):
        return {"tensor": xh * ny + i}

    def xdev(i):
        return {"dp": i, "tensor": (1 - xh) * ny + y}

    def at_y(rel):
        return (y + rel + ny) % ny

    def at_z(rel):
        return (z + rel + nz) % nz

    barrier = pltpu.get_barrier_semaphore()
    greeted = [zdev(at_z(k)) for k in range(1, nz)]
    greeted += [xpeer]
    greeted += [ydev(at_y(1)), ydev(at_y(-1)), other_core, next_chip]
    for device in greeted:
        pl.semaphore_signal(barrier, inc=1, device_id=device, device_id_type=MESH)

    pairs = [
        (out_grad_hbm, out_grad),
        (stash_hbm, stash),
        (attn_in_hbm, attn_in),
        (seg_hbm, seg),
        (weight_hbm, weight),
        (lens_hbm, lens),
        (resid_hbm, resid),
    ]
    loads = [pltpu.make_async_copy(a, b, local_sems.at[i]) for i, (a, b) in enumerate(pairs)]
    for load in loads:
        load.start()
    loads[0].wait()

    pool = Pool(sems)
    groups = []

    def sends(view, device):
        groups.append(Sends(pool, view, device))
        return groups[-1]

    for d in range(nz):
        b1s[d] = to_tall(out_grad[:, d * C : (d + 1) * C].astype(F32)).astype(BF16)
    b1r[z] = b1s[z]

    pl.semaphore_wait(barrier, len(greeted))

    some_z = zdev(at_z(1))
    some_y = ydev(at_y(1))
    b1 = sends(b1r.at[pl.ds(0, nz - 1)], some_z)
    b1_recv = pool.new()
    for k in (4, 3, -3, 2, -2, 1, -1):
        b1.send(b1s.at[at_z(k)], b1r.at[z], zdev(at_z(k)), b1_recv)

    def permuted(x):
        return [
            jnp.concatenate(
                [x[h * ny * ROWS + b * ROWS : h * ny * ROWS + (b + 1) * ROWS] for h in (0, 1)],
                axis=0,
            )
            for b in range(ny)
        ]

    def natural(x):
        return jnp.concatenate(
            [x[(2 * b + h) * ROWS : (2 * b + h + 1) * ROWS] for h in (0, 1) for b in range(ny)],
            axis=0,
        )

    loads[1].wait()
    slot = fetch[0, 0]
    held = stash[slot]
    for b, rows in enumerate(permuted(held[:, W_IN:].astype(F32))):
        reto[b] = rows.astype(BF16)
    retq[...] = held[:, :W_IN]

    def across_core(src, via):
        return sends(src, other_core).send(src, via, other_core)

    def to_mirror(via, dst):
        return sends(via, next_chip).send(via, dst, next_chip)

    core_o = across_core(reto, reto_via)
    core_q = across_core(retq, retq_via)

    loads[2].wait()
    core_p = across_core(attn_in, evp_via)
    loads[3].wait()
    row_id = lax.broadcasted_iota(jnp.int32, (tok, tok), 0)
    col_id = lax.broadcasted_iota(jnp.int32, (tok, tok), 1)
    seg_cols = jnp.broadcast_to(seg[...].astype(F32), (tok, tok))
    allowed = (seg_cols == jnp.transpose(seg_cols)) & (col_id <= row_id)
    q = stack_heads(attn_in[:, :QW], heads)
    k = attn_in[:, QW : QW + HEAD]
    v = attn_in[:, QW + HEAD : W_IN]
    weights = probabilities(q, k, allowed, heads).astype(BF16)
    att = unstack_heads(dot(weights, v), heads)
    attb[...] = att.astype(BF16)
    core_a = across_core(attb, eva_via)
    for b, rows in enumerate(permuted(att)):
        A[0, b] = rows.astype(BF16)


    def two_way(parts):
        return [
            (way, p, 4 if (p < parts // 2) == (way == 1) else 3)
            for p in range(parts)
            for way in (1, -1)
        ]

    def a_piece(rel, h):
        return A.at[NEAR.index(rel), pl.ds(h * ny // A_PARTS, ny // A_PARTS)]

    def ring_rel(rel):
        return 4 if rel == -4 else rel

    gather_a = Gather(
        sends(A.at[pl.ds(0, nz - 1)], some_z),
        nz,
        z,
        zdev,
        two_way(A_PARTS),
        lambda way, h, r: a_piece(ring_rel(-way * r), h),
        lambda way, h, r: a_piece(ring_rel(-way * (r + 1)), h),
    )

    def o_piece(way, h, r):
        return O.at[at_z(-way * r), pl.ds(h * ny // O_PARTS, ny // O_PARTS)]

    gather_o = Gather(
        sends(O.at[pl.ds(0, nz - 1)], some_z), nz, z, zdev, two_way(O_PARTS), o_piece, o_piece
    )

    sub = nz * ROWS // G_PARTS

    def g_piece(way, h, r):
        return G.at[at_y(-way * r), xh, pl.ds(h * sub, sub)]

    gather_g = Gather(
        sends(G.at[pl.ds(0, ny - 1), 0], some_y), ny, y, ydev, two_way(G_PARTS), g_piece, g_piece
    )

    def other_piece(way, h, r):
        return G.at[at_y(-way * r), 1 - xh]

    gather_other = Gather(
        sends(G.at[pl.ds(0, 2 * X_HOPS), 0], some_y),
        ny,
        y,
        ydev,
        ((1, 0, X_HOPS), (-1, 0, X_HOPS)),
        other_piece,
        other_piece,
    )
    across = [0] + [rel for rel in NEAR if abs(rel) > X_HOPS]
    g_x = sends(G.at[pl.ds(0, len(across)), 0], xpeer)
    g_x_moves = {}

    def send_across(rel):
        ref = G.at[at_y(rel), xh]
        g_x_moves[rel] = g_x.send(ref, ref, xpeer)

    gather_a.step(0)

    def cotangent_piece(group, recv, h, at):
        group.whole(recv).wait_recv()
        for p in range(nz // 2):
            rows = [to_wide(b1r[h * nz + 2 * p + j].astype(F32)) for j in (0, 1)]
            G[y, at, pl.ds(2 * ROWS * p, 2 * ROWS), :] = jnp.concatenate(rows, axis=0).astype(BF16)

    cotangent_piece(b1, b1_recv, 0, xh)
    gather_g.step(0)
    send_across(0)
    gather_a.step(1)

    for load in loads[4:]:
        load.wait()

    Z_SPLIT = ((0, 5, 3), (5, 3, 2))
    z_sums = []
    for lo, count, cut in Z_SPLIT:
        z_sums.append(
            RingSum(
                sends(O.at[pl.ds(0, nz - 1), pl.ds(0, count)], some_z),
                z,
                nz,
                zdev,
                lambda side, r, lo=lo, count=count: zslots.at[side, r, pl.ds(lo, count)],
                ((0, cut), (cut, count - cut)),
            )
        )

    def head_grad_part(rels):
        for rel in rels:
            b = at_y(rel)
            res = dot(G[b].reshape(2 * nz * ROWS, C), weight[...], 1, 1)
            for d in range(nz):
                both = [res[(h * nz + d) * ROWS : (h * nz + d + 1) * ROWS] for h in (0, 1)]
                part[d, NEAR.index(rel)] = jnp.concatenate(both, axis=0).astype(BF16)

    def head_grad_step(i, r):
        lo, count, _ = Z_SPLIT[i]
        z_sums[i].step(r, lambda rel: part[at_z(rel), pl.ds(lo, count)].astype(F32))

    RUNS = nz // 2
    y_sums = [
        RingSum(
            sends(G.at[pl.ds(0, ny - 1), 0], some_y),
            y,
            ny,
            ydev,
            lambda side, r, g=g: yslots.at[g, side, r],
            ((0, RUNS * ROWS), (RUNS * ROWS, RUNS * ROWS)),
        )
        for g in (0, 1)
    ]

    def branch_term(g, rel):
        rows = A[pl.ds(g * RUNS, RUNS), at_y(rel)].reshape(RUNS * 2 * ROWS, QW)
        return dot(rows, weight[...])

    def branch_step(g, r):
        y_sums[g].step(r, lambda rel: branch_term(g, rel))

    f5 = sends(f5r.at[pl.ds(0, nz - 1)], some_z)
    f5_recv = pool.new()
    keep, x_moves = {}, {}

    def branch_x(g):
        total = branch_term(g, 0) + y_sums[g].last()
        halves = [
            jnp.concatenate(
                [total[(2 * j + h) * ROWS : (2 * j + h + 1) * ROWS] for j in range(RUNS)], axis=0
            )
            for h in (0, 1)
        ]
        xs[g] = jnp.where(xh == 0, halves[1], halves[0]).astype(BF16)
        x_moves[g] = sends(xs.at[g], xpeer).send(xs.at[g], xr.at[g], xpeer)
        keep[g] = jnp.where(xh == 0, halves[0], halves[1])

    def branch_end(g):
        x_moves[g].wait_recv()
        total = keep[g] + xr[g].astype(F32)
        for j in reversed(range(RUNS)):
            slot = g * RUNS + j
            rel = NEAR[slot]
            tall = to_tall(total[j * ROWS : (j + 1) * ROWS]).astype(BF16)
            if rel == 0:
                f5r[z] = tall
            else:
                f5s[slot] = tall
                f5.send(f5s.at[slot], f5r.at[z], zdev(at_z(rel)), f5_recv)

    def weight_grad_part(i):
        cols = pl.ds(i * (C // 4), C // 4)
        wgrad_out[:, cols] = dot(
            OT[...], G[:, :, :, cols].reshape(nt * nz * ROWS, C // 4)
        ).astype(BF16)

    def arrange_outputs():
        for b in range(ny):
            x = O[:, b].astype(F32)
            rows = [x[d, h * ROWS : (h + 1) * ROWS] for h in (0, 1) for d in range(nz)]
            block = jnp.concatenate(rows, axis=0)
            width = 2 * nz * ROWS
            OT[:, b * width : (b + 1) * width] = jnp.transpose(block).astype(BF16)

    gather_g.step(1)
    g_x_moves[0].wait_recv()
    gather_other.step(0)
    core_o.wait_recv()
    move_ret_o = to_mirror(reto_via, O.at[z])
    gather_a.step(2)
    head_grad_part((0,))
    branch_step(0, 0)
    gather_g.step(2)
    send_across(2)
    send_across(-2)
    gather_other.step(1)
    gather_a.step(3)
    head_grad_part((1, -1))
    branch_step(0, 1)
    gather_g.step(3)
    send_across(3)
    send_across(-3)
    move_ret_o.wait_recv()
    gather_o.step(0)
    g_x_moves[2].wait_recv()
    g_x_moves[-2].wait_recv()
    head_grad_part((2, -2))
    head_grad_step(0, 0)
    gather_a.step(4)
    branch_step(1, 0)
    branch_step(0, 2)
    gather_g.step(4)
    send_across(4)
    gather_o.step(1)
    head_grad_step(0, 1)
    branch_step(1, 1)
    g_x_moves[3].wait_recv()
    g_x_moves[-3].wait_recv()
    head_grad_part((3, -3))
    branch_step(0, 3)
    g_x_moves[4].wait_recv()
    head_grad_part((4,))
    head_grad_step(1, 0)
    core_q.wait_recv()
    move_ret_q = to_mirror(retq_via, retr)
    gather_o.step(2)
    head_grad_step(0, 2)
    branch_step(1, 2)
    head_grad_step(1, 1)
    core_p.wait_recv()
    core_a.wait_recv()
    move_ev_p = to_mirror(evp_via, evp)
    move_ev_a = to_mirror(eva_via, eva)
    branch_x(0)
    gather_o.step(3)
    head_grad_step(0, 3)
    branch_step(1, 3)
    head_grad_step(1, 2)
    branch_end(0)
    head_grad_step(1, 3)
    branch_x(1)

    move_ret_q.wait_recv()
    end = jnp.int32(0)
    seg_row = jnp.zeros((tok, tok), jnp.int32)
    seg_col = jnp.zeros((tok, tok), jnp.int32)
    for c in range(lens.shape[1]):
        end = end + lens[0, c]
        seg_row += (row_id >= end).astype(jnp.int32)
        seg_col += (col_id >= end).astype(jnp.int32)
    allowed = (seg_row == seg_col) & (col_id <= row_id)
    q = stack_heads(retr[:, :QW], heads)
    k = retr[:, QW : QW + HEAD]
    v = retr[:, QW + HEAD : W_IN]
    probs = probabilities(q, k, allowed, heads)
    old = natural(O[z].astype(F32).reshape(tok, QW))

    branch_end(1)

    sums = jnp.concatenate([z_sums[0].last(), z_sums[1].last()], axis=0)
    total = part[z].astype(F32) + sums
    for j, rel in enumerate(NEAR):
        for h in (0, 1):
            row = pl.multiple_of((h * ny + at_y(rel)) * ROWS, ROWS)
            dnat[pl.ds(row, ROWS), :] = total[j, h * ROWS : (h + 1) * ROWS]
    d_out = dnat[...].astype(BF16)
    d_heads = stack_heads(d_out, heads)
    grad_v = dot(probs.astype(BF16), d_heads, 0, 0)
    grad_p = dot(d_heads, v, 1, 1)
    inner = jnp.sum(d_heads.astype(F32) * stack_heads(old, heads), axis=-1, keepdims=True)
    grad_s = (probs * (grad_p - inner)).astype(BF16)
    grad_k = dot(grad_s, q, 0, 0) * HEAD ** (-0.5)
    shs[:, :HEAD] = grad_k.astype(BF16)
    shs[:, HEAD:] = grad_v.astype(BF16)
    move_shared = sends(shs, pair).send(shs, shr, pair)
    grad_q = dot(grad_s, k) * HEAD ** (-0.5)
    agrad_out[:, :QW] = unstack_heads(grad_q, heads).astype(BF16)
    gather_o.step(4)
    arrange_outputs()
    for i in range(4):
        weight_grad_part(i)
    move_ev_p.wait_recv()
    move_ev_a.wait_recv()
    for i in range(stash.shape[0]):
        here = evict[0] == i
        stash_out[i, :, :W_IN] = jnp.where(here, evp[...], stash[i, :, :W_IN])
        stash_out[i, :, W_IN:] = jnp.where(here, eva[...], stash[i, :, W_IN:])

    move_shared.wait_recv()
    agrad_out[:, QW:] = (shs[...].astype(F32) + shr[...].astype(F32)).astype(BF16)

    f5.whole(f5_recv).wait_recv()
    for d in range(nz):
        cols = slice(d * C, (d + 1) * C)
        summed = to_wide(f5r[d].astype(F32))
        lay_out[:, cols] = (resid[:, cols].astype(F32) + summed).astype(BF16)

    for group in groups:
        group.finish()


def body(
    dims,
    resid_in,
    attn_in,
    seg_fwd,
    out_weight,
    stash_held,
    len_bwd,
    out_grad,
    evict_slot,
    fetch_slot,
):
    n_sec, nz, nt = dims
    ny = nt // 2
    tok = nt * ROWS
    QW, C = out_weight.shape[1:]
    D = resid_in.shape[-1]
    W_IN = QW + 2 * HEAD
    slots, width = stash_held.shape[1], stash_held.shape[-1]
    vmem, smem, hbm = (
        pl.BlockSpec(memory_space=s) for s in (pltpu.VMEM, pltpu.SMEM, pltpu.HBM)
    )

    def buf(*shape):
        return pltpu.VMEM(shape, BF16)

    outs = pl.pallas_call(
        functools.partial(kernel, dims),
        out_shape=(
            jax.ShapeDtypeStruct((ROWS, D), BF16),
            jax.ShapeDtypeStruct((slots, tok, width), BF16),
            jax.ShapeDtypeStruct((QW, C), BF16),
            jax.ShapeDtypeStruct((tok, W_IN), BF16),
        ),
        in_specs=[hbm] * 7 + [smem] * 2,
        out_specs=(vmem,) * 4,
        scratch_shapes=[
            buf(ROWS, D),
            buf(tok, W_IN),
            pltpu.VMEM((1, tok), jnp.int32),
            pltpu.SMEM(len_bwd.shape[1:], jnp.int32),
            buf(QW, C),
            buf(slots, tok, width),
            buf(ROWS, D),
            buf(nz, 2 * ROWS, C // 2),
            buf(2 * nz, 2 * ROWS, C // 2),
            buf(ny, 2, nz * ROWS, C),
            buf(nz, ny, 2 * ROWS, QW),
            buf(2, nz // 2 + 1, ny, 2 * ROWS, QW),
            buf(nz, ny, 2 * ROWS, QW),
            buf(nz, ny, 2 * ROWS, QW),
            buf(2, 2, ny // 2 + 1, nz * ROWS, C),
            buf(nz, 2 * ROWS, C // 2),
            buf(nz, 2 * ROWS, C // 2),
            buf(2, nz // 2 * ROWS, C),
            buf(2, nz // 2 * ROWS, C),
            buf(tok, QW),
            buf(ny, 2 * ROWS, QW),
            buf(ny, 2 * ROWS, QW),
            buf(tok, W_IN),
            buf(tok, W_IN),
            buf(tok, W_IN),
            buf(tok, W_IN),
            buf(tok, W_IN),
            buf(tok, QW),
            buf(tok, QW),
            buf(tok, 2 * HEAD),
            buf(tok, 2 * HEAD),
            buf(QW, nt * nz * ROWS),
            pltpu.VMEM((tok, QW), F32),
            pltpu.SemaphoreType.DMA((SEMS,)),
            pltpu.SemaphoreType.DMA((7,)),
        ],
        compiler_params=pltpu.CompilerParams(
            collective_id=0, has_side_effects=True, vmem_limit_bytes=48 * 2**20
        ),
    )(
        *(
            pltpu.with_memory_space_constraint(x, pltpu.HBM) if x.size > 1 else x
            for x in (
                resid_in[0],
                attn_in[0],
                seg_fwd[0],
                len_bwd[0],
                out_weight[0],
                stash_held[0],
                out_grad[0],
                evict_slot,
                fetch_slot,
            )
        )
    )
    return tuple(x[None] for x in outs)


def solution(mesh):
    dims = tuple(mesh.shape[a] for a in ("section", "dp", "tensor"))
    placed = (
        P("section", ("dp", "tensor"), None),
        P("section", "dp", "tensor"),
        P("section", "dp", None),
        P("section", "tensor", "dp"),
        P("section", None, "dp", "tensor"),
        P("section", "dp", None),
        P("section", ("dp", "tensor"), None),
        P("section"),
        P("section", "dp"),
    )
    return jax.shard_map(
        functools.partial(body, dims),
        mesh=mesh,
        in_specs=placed,
        out_specs=(
            P("section", ("dp", "tensor"), None),
            P("section", None, "dp", "tensor"),
            P("section", "tensor", "dp"),
            P("section", "dp", "tensor"),
        ),
        check_vma=False,
    )
```
